32 devices in a mesh: slab: 8 (over z, core), col: 4 (over y, x).
Axes of the slice: x: 2, y: 2, z: 4, core: 2. Of those that a mesh axis runs over, the one named last changes fastest.
Arguments:
- sensitivity: bfloat16 [3, 512, 32768], P(None, 'col', 'slab'), may hold values from -0.046875 to 0.046875
- residual_force: bfloat16 [3, 32768], P(None, 'slab'), may hold values from -6 to 6
- moments: float32 [6, 32, 1024], P(None, 'slab'), as said below
- zone_label: int32 [32, 1024], P('slab'), may hold values from 0 to 511, as said below
- misfit: float32 [32, 1024], P('slab'), may hold values from 0.1 to 10
Outputs:
- hessian: float32 [512, 512], P('col', 'slab')
- gradient: float32 [512], replicated
- zone_misfit: float32 [512], replicated
The draws below stay inside these ranges and needn't reach their ends.
Inputs may be any that keep to these rules, and one draw needn't show every extreme that they name: zone_label is the box of a 8 x 8 x 8 partition of the specimen that holds the element, the in-plane box borders displaced by at most one element; every zone occurs. `moments`: each element's moment matrix is symmetric with positive diagonal, and each diagonal entry exceeds the sum of the magnitudes of the others in its row.
All inputs are finite; a program needn't handle non-finite values.
Results may differ from the reference program's by a relative error of at most 0.0003.
Values may be sent and summed in bfloat16 or wider, within the bound.
No kernel may reach another device: no remote copies, remote signals or barrier semaphores. Data moves between devices by JAX's collectives and lax.ppermute only.
A program may use at most 128 MiB of HBM per device.

```python
import math
import jax
import jax.numpy as jnp
from jax import lax

GX = 64
GY = 16
ZB = 8
P_SIZE = 512
NLAYERS = 32
NODES = 32768


def draw_moments(key, part):
    count = NLAYERS * GX * GY
    keys = jax.random.split(key, 2)
    diag = jnp.exp(jax.random.uniform(keys[0], (3, count), jnp.float32, math.log(0.5), math.log(2.0)))
    coupling = jax.random.uniform(keys[1], (3, count), jnp.float32, -0.45, 0.45)
    off_xy = coupling[0] * jnp.minimum(diag[0], diag[1])
    off_xz = coupling[1] * jnp.minimum(diag[0], diag[2])
    off_yz = coupling[2] * jnp.minimum(diag[1], diag[2])
    whole = jnp.concatenate([diag, jnp.stack([off_xy, off_xz, off_yz])], axis=0)
    return whole.reshape(6, NLAYERS, GX * GY)


def draw_zone_label(key, part):
    keys = jax.random.split(key, 2)
    layer = jnp.arange(NLAYERS, dtype=jnp.int32)[:, None]
    cell = jnp.arange(GX * GY, dtype=jnp.int32)[None, :]
    pos_x = cell // GY
    pos_y = cell % GY
    wide_x = GX // ZB
    wide_y = GY // ZB
    shape = (NLAYERS, GX * GY)
    jitter_x = jax.random.randint(keys[0], shape, -1, 2, jnp.int32) * (pos_x % wide_x != 0).astype(jnp.int32)
    jitter_y = jax.random.randint(keys[1], shape, -1, 2, jnp.int32) * (pos_y % wide_y != 0).astype(jnp.int32)
    box_x = jnp.clip(pos_x + jitter_x, 0, GX - 1) // wide_x
    box_y = jnp.clip(pos_y + jitter_y, 0, GY - 1) // wide_y
    box_z = layer // (NLAYERS // ZB) + jnp.zeros(shape, jnp.int32)
    return ((box_z * ZB + box_x) * ZB + box_y).astype(jnp.int32)


def block_levels(rng, dims, cuts, least, top_value):
    level, own = 1.0, jax.random.fold_in(rng, 6)
    for position, shards_of in cuts:
        heights = jnp.exp(jax.random.uniform(jax.random.fold_in(own, position), (shards_of,), jnp.float32, least / len(cuts), top_value / len(cuts)))
        level = level * jnp.repeat(heights, dims[position] // shards_of).reshape([-1 if axis == position else 1 for axis in range(len(dims))])
    return level


def bell_draw(key, dims, scale, bound, shards=(), kind=jnp.bfloat16):
    result = jax.random.normal(key, dims, jnp.float32) * scale
    if len(shards) > 0:
        result = block_levels(key, dims, shards, -0.22, 0.18) * result
    return jnp.clip(result, min=-bound, max=bound).astype(kind)


def setup_inputs(seed: int = 0) -> dict:
    arg_keys = jax.random.split(jax.random.key(seed), 6)
    sensitivity = bell_draw(arg_keys[0], (3, P_SIZE, NODES), ((3 * NODES) ** -0.5), 0.046875, ((1, 4), (2, 8)))
    residual_force = bell_draw(arg_keys[1], (3, NODES), 1.0, 6.0, ((1, 8),))
    moments = draw_moments(jax.random.fold_in(arg_keys[5], 71), 0)
    zone_label = draw_zone_label(jax.random.fold_in(arg_keys[5], 71), 0)
    misfit = jnp.clip(jnp.exp(math.log(10.0) - 4.6051702 * jax.random.uniform(arg_keys[4], (NLAYERS, GX * GY), jnp.float32) ** block_levels(arg_keys[4], (NLAYERS, GX * GY), ((0, 8),), -0.2, 0.2)), 0.1, 10.0)
    return {"sensitivity": sensitivity, "residual_force": residual_force, "moments": moments, "zone_label": zone_label, "misfit": misfit}


third = 1.0 / 3.0
sixth = 1.0 / 6.0


def mix_pair(first, second):
    return third * first + sixth * second, sixth * first + third * second


def shift_ahead(field, step, keep):
    moved = jnp.concatenate([field[..., step:], jnp.zeros_like(field[..., :step])], axis=-1)
    if keep is None:
        return moved
    return jnp.where(keep, moved, 0.0)


def shift_behind(field, step, keep):
    moved = jnp.concatenate([jnp.zeros_like(field[..., :step]), field[..., :-step]], axis=-1)
    if keep is None:
        return moved
    return jnp.where(keep, moved, 0.0)


def apply_moments(moments, field):
    comps = [moments[k][None, :] for k in range(6)]
    first, second, last = field[0], field[1], field[2]
    out_x = comps[0] * first + comps[3] * second + comps[4] * last
    out_y = comps[3] * first + comps[1] * second + comps[5] * last
    out_z = comps[4] * first + comps[5] * second + comps[2] * last
    return jnp.stack([out_x, out_y, out_z])


def element_layer(lower, upper, moments):
    plane = lower.shape[-1]
    pos_y = jnp.arange(plane, dtype=jnp.int32) % GY
    not_last = pos_y != GY - 1
    not_first = pos_y != 0
    mixed_z = mix_pair(lower, upper)
    results = []
    for side_z in range(2):
        field = mixed_z[side_z]
        mixed_x = mix_pair(field, shift_ahead(field, GY, None))
        values = []
        for side_x in range(2):
            layer = mixed_x[side_x]
            mixed_y = mix_pair(layer, shift_ahead(layer, 1, not_last))
            values.append([apply_moments(moments, mixed_y[side_y]) for side_y in range(2)])
        total = values[0][0]
        total = total + shift_behind(values[1][0], GY, None)
        total = total + shift_behind(values[0][1], 1, not_first)
        total = total + shift_behind(shift_behind(values[1][1], 1, not_first), GY, None)
        results.append(total)
    return results[0], results[1]


def reference(sensitivity, residual_force, moments, zone_label, misfit):
    cols = sensitivity.shape[1]
    layers = moments.shape[1]
    plane = GX * GY
    field = sensitivity.reshape(3, cols, layers, plane)

    def one_layer(level):
        lower = lax.dynamic_index_in_dim(field, level, 2, keepdims=False).astype(jnp.float32)
        above_index = jnp.minimum(level + 1, layers - 1).astype(jnp.int32)
        upper = lax.dynamic_index_in_dim(field, above_index, 2, keepdims=False).astype(jnp.float32)
        upper = jnp.where(level + 1 < layers, upper, jnp.zeros_like(upper))
        layer_moments = lax.dynamic_index_in_dim(moments, level, 1, keepdims=False)
        return element_layer(lower, upper, layer_moments)

    to_lower, to_upper = lax.map(one_layer, jnp.arange(layers, dtype=jnp.int32))
    from_below = jnp.concatenate([jnp.zeros_like(to_upper[:1]), to_upper[:-1]], axis=0)
    stacked = (from_below + to_lower).astype(jnp.bfloat16)
    image = jnp.moveaxis(stacked, 0, 2).reshape(3, cols, layers * plane)
    hessian = lax.dot_general(image, sensitivity, (((0, 2), (0, 2)), ((), ())), preferred_element_type=jnp.float32)
    gradient = lax.dot_general(residual_force, sensitivity, (((0, 1), (0, 2)), ((), ())), preferred_element_type=jnp.float32)
    total = zone_label.size
    sums = jax.ops.segment_sum(misfit.reshape(-1), zone_label.reshape(-1), num_segments=cols)
    zone_misfit = sums * (cols / total)
    return hessian, gradient, zone_misfit
```

```python
import functools

import jax
import jax.numpy as jnp
from jax import lax
from jax.experimental import pallas as pl
from jax.experimental.pallas import tpu as pltpu
from jax.sharding import PartitionSpec as P

GX = 64
GY = 16
TILE = 128
ROWS = 16


def exchange(value, axis, by):
    count = lax.axis_size(axis)
    return lax.ppermute(value, axis, [(i, i ^ by) for i in range(count)])


def shifted(value, axis, by):
    count = lax.axis_size(axis)
    pairs = [(i, i + by) for i in range(count) if 0 <= i + by < count]
    return lax.ppermute(value, axis, pairs)


def lane_of(shape):
    return lax.broadcasted_iota(jnp.int32, shape, 1)


def pack_kernel(layers, width, last, target, *refs):
    planes, edges = refs[:layers], refs[layers : 2 * layers]
    first_ref, rest_ref = refs[2 * layers :]
    inside = target[0] != last
    for k in range(3):
        first_ref[k, :, :width] = planes[0][k]
        for level in range(1, layers):
            rest_ref[k, :, (level - 1) * width : level * width] = planes[level][k]
        rows = first_ref.shape[1]
        lane = lane_of((rows, TILE))
        halo = jnp.zeros((rows, TILE), jnp.float32)
        for level in range(layers):
            edge = edges[level][k].astype(jnp.float32)
            at = GY * level
            if at:
                edge = pltpu.roll(edge, at, 1)
            halo = jnp.where((lane >= at) & (lane < at + GY) & inside, edge, halo)
        first_ref[k, :, width:] = halo.astype(first_ref.dtype)


def pack(sensitivity, target, layers, plane, n_col):
    cols = sensitivity.shape[1]
    width = plane // n_col
    top_block = layers * plane // TILE - 1

    def plane_spec(level):
        return pl.BlockSpec((3, cols, width), lambda i, t: (0, 0, level * n_col + t[0]))

    def edge_spec(level):
        def place(i, t):
            block = (level * plane + (t[0] + 1) * width) // TILE
            return (0, 0, jnp.minimum(block, top_block))

        return pl.BlockSpec((3, cols, TILE), place)

    first = jax.ShapeDtypeStruct((3, cols, width + TILE), sensitivity.dtype)
    rest = jax.ShapeDtypeStruct((3, cols, (layers - 1) * width), sensitivity.dtype)
    return pl.pallas_call(
        functools.partial(pack_kernel, layers, width, n_col - 1),
        grid_spec=pltpu.PrefetchScalarGridSpec(
            num_scalar_prefetch=1,
            grid=(1,),
            in_specs=[plane_spec(l) for l in range(layers)] + [edge_spec(l) for l in range(layers)],
            out_specs=[
                pl.BlockSpec(first.shape, lambda i, t: (0, 0, 0)),
                pl.BlockSpec(rest.shape, lambda i, t: (0, 0, 0)),
            ],
        ),
        out_shape=[first, rest],
        compiler_params=pltpu.CompilerParams(vmem_limit_bytes=24 << 20),
        cost_estimate=pl.CostEstimate(flops=0, bytes_accessed=2 << 20, transcendentals=0),
        name="pack",
    )(target, *([sensitivity] * (2 * layers)))


def stencil_half(planes, halo, top_halo, coef, layers, width):
    wide = lane_of((8, width))
    tile = lane_of((8, TILE))
    wide_y, tile_y = wide % GY, tile % GY
    zero = jnp.zeros((), jnp.float32)

    def mix_y(field, pos):
        ahead = jnp.where(pos != GY - 1, pltpu.roll(field, field.shape[1] - 1, 1), zero)
        total = field + ahead
        return field + total, ahead + total

    halo_mixed = [mix_y(halo[k], tile_y) for k in range(3)]
    top_mixed = [mix_y(top_halo[k], tile_y) for k in range(3)]

    def plane_fields(level):
        result = []
        for k in range(3):
            columns = []
            for side_y, field in enumerate(mix_y(planes[level][k], wide_y)):
                if level < layers:
                    edge, at = halo_mixed[k][side_y], GY * level
                else:
                    edge, at = top_mixed[k][side_y], 0
                edge = pltpu.roll(edge, (TILE - GY - at) % TILE, 1) if (TILE - GY - at) % TILE else edge
                ahead = pltpu.roll(field, width - GY, 1)
                tail = jnp.where(tile >= TILE - GY, edge, ahead[:, width - TILE :])
                if width > TILE:
                    ahead = jnp.concatenate([ahead[:, : width - TILE], tail], axis=1)
                else:
                    ahead = tail
                total = field + ahead
                columns.append((field + total, ahead + total))
            result.append(columns)
        return result

    def gather(fields, at, edge_sum):
        images, edges = [], []
        for k in range(3):
            sums, tiles = [], []
            for side_y in range(2):
                near, far = fields[k][side_y]
                moved = pltpu.roll(far, GY, 1)
                sums.append(near + jnp.where(wide >= GY, moved, zero))
                tail = far[:, width - TILE :]
                turn = (GY + at) % TILE
                tail = pltpu.roll(tail, turn, 1) if turn else tail
                tiles.append(jnp.where((tile >= at) & (tile < at + GY), tail, edge_sum[k][side_y]))
            images.append(sums[0] + jnp.where(wide_y != 0, pltpu.roll(sums[1], 1, 1), zero))
            edges.append(tiles)
        return images, edges

    def edge_image(edges):
        return [e[0] + jnp.where(tile_y != 0, pltpu.roll(e[1], 1, 1), zero) for e in edges]

    blank = jnp.zeros((8, TILE), jnp.float32)
    edge_sum = [[blank, blank] for _ in range(3)]
    images = []
    lower = plane_fields(0)
    carry = None
    for level in range(layers):
        upper = plane_fields(level + 1)
        here = [[[None, None], [None, None]] for _ in range(3)]
        above = [[[None, None], [None, None]] for _ in range(3)]
        g = [coef(k, level) for k in range(6)]
        for side_y in range(2):
            for side_x in range(2):
                low, top = [], []
                for k in range(3):
                    a, b = lower[k][side_y][side_x], upper[k][side_y][side_x]
                    total = a + b
                    low.append(a + total)
                    top.append(b + total)
                for out, f in ((here, low), (above, top)):
                    out[0][side_y][side_x] = g[0] * f[0] + g[3] * f[1] + g[4] * f[2]
                    out[1][side_y][side_x] = g[3] * f[0] + g[1] * f[1] + g[5] * f[2]
                    out[2][side_y][side_x] = g[4] * f[0] + g[5] * f[1] + g[2] * f[2]
                if carry is not None:
                    for k in range(3):
                        here[k][side_y][side_x] = here[k][side_y][side_x] + carry[k][side_y][side_x]
        image, edge_sum = gather(here, GY * level, edge_sum)
        images.append(image)
        carry = above
        lower = upper
    image, top_edges = gather(carry, 0, [[blank, blank] for _ in range(3)])
    images.append(image)
    return images, edge_image(edge_sum), edge_image(top_edges)


def image_kernel(layers, width, place, first_ref, rest_ref, top_ref, moments_ref, *refs):
    values_ref, image_ref, coef_ref = refs[-3:]
    for level in range(layers):
        for k in range(6):
            row = moments_ref[k, level : level + 1, :] * (1.0 / 216.0)
            coef_ref[k, level] = jnp.broadcast_to(row, (8, width))
    tops = width + TILE + (layers - 1) * width

    def body(step, _):
        rows = pl.ds(pl.multiple_of(step * ROWS, ROWS), ROWS)
        first = [first_ref[k, rows, :] for k in range(3)]
        rest = [rest_ref[k, rows, :] for k in range(3)]
        top = [top_ref[k, rows, :] for k in range(3)]
        for k in range(3):
            values_ref[k, rows, : width + TILE] = first[k]
            values_ref[k, rows, width + TILE : tops] = rest[k]
            values_ref[k, rows, tops:] = top[k]
        halves = []
        for half in range(2):
            part = slice(8 * half, 8 * half + 8)
            f32 = jnp.float32
            planes = [[first[k][:, :width].astype(f32)[part] for k in range(3)]]
            for level in range(layers - 1):
                cut = slice(level * width, (level + 1) * width)
                planes.append([rest[k][:, cut].astype(f32)[part] for k in range(3)])
            planes.append([top[k][:, :width].astype(f32)[part] for k in range(3)])
            halo = [first[k][:, width:].astype(f32)[part] for k in range(3)]
            top_halo = [top[k][:, width:].astype(f32)[part] for k in range(3)]
            halves.append(
                stencil_half(planes, halo, top_halo, lambda k, level: coef_ref[k, level], layers, width)
            )

        def put(k, start, size, low, high):
            image_ref[k, rows, start : start + size] = jnp.concatenate([low, high], axis=0).astype(image_ref.dtype)

        for k in range(3):
            (im0, e0, t0), (im1, e1, t1) = halves
            put(k, 0, width, im0[0][k], im1[0][k])
            put(k, width, TILE, e0[k], e1[k])
            for level in range(1, layers + 1):
                start = width + TILE + (level - 1) * width
                put(k, start, width, im0[level][k], im1[level][k])
            put(k, tops + width, TILE, t0[k], t1[k])
        return 0

    lax.fori_loop(0, first_ref.shape[1] // ROWS, body, 0)


def image_piece(index, place, first, rest, top, moments, buffers, n_col):
    cols, width = first.shape[1], first.shape[2] - TILE
    layers = rest.shape[2] // width + 1
    block = min(cols, 32)
    steps = cols // block
    total = 2 * (width + TILE) + (layers - 1) * width
    shape = jax.ShapeDtypeStruct((3, cols * n_col, total), first.dtype)
    in_specs = [
        pl.BlockSpec((3, block, width + TILE), lambda i, t: (0, i, 0)),
        pl.BlockSpec((3, block, (layers - 1) * width), lambda i, t: (0, i, 0)),
        pl.BlockSpec((3, block, width + TILE), lambda i, t: (0, i, 0)),
        pl.BlockSpec((6, layers, width), lambda i, t: (0, 0, t[0])),
    ]
    args = [place, first, rest, top, moments]
    aliases = {}
    if buffers is not None:
        in_specs += [pl.BlockSpec(memory_space=pl.ANY)] * 2
        args += list(buffers)
        aliases = {5: 0, 6: 1}
    work = cols * (layers * width) * 3 * 100
    return pl.pallas_call(
        functools.partial(image_kernel, layers, width),
        grid_spec=pltpu.PrefetchScalarGridSpec(
            num_scalar_prefetch=1,
            grid=(steps,),
            in_specs=in_specs,
            out_specs=[
                pl.BlockSpec((3, block, total), lambda i, t: (0, t[1] * steps + i, 0)),
                pl.BlockSpec((3, block, total), lambda i, t: (0, index * steps + i, 0)),
            ],
            scratch_shapes=[pltpu.VMEM((6, layers, 8, width), jnp.float32)],
        ),
        out_shape=[shape, shape],
        input_output_aliases=aliases,
        compiler_params=pltpu.CompilerParams(vmem_limit_bytes=24 << 20),
        cost_estimate=pl.CostEstimate(flops=work, bytes_accessed=4 << 20, transcendentals=0),
        name="image",
    )(*args)


def hessian_kernel(blocks, half, core, values_ref, image_ref, keep_ref, send_ref, total):
    step = pl.program_id(0)

    @pl.when(step == 0)
    def _():
        total[...] = jnp.zeros_like(total)

    total[...] += lax.dot_general(
        values_ref[0], image_ref[0], (((1,), (1,)), ((), ())), preferred_element_type=jnp.float32
    )

    @pl.when(step == pl.num_programs(0) - 1)
    def _():
        for b in range(blocks):
            lo = total[2 * b * half : (2 * b + 1) * half, :]
            hi = total[(2 * b + 1) * half : (2 * b + 2) * half, :]
            keep_ref[b * half : (b + 1) * half, :] = jnp.where(core[0] == 0, lo, hi)
            send_ref[b * half : (b + 1) * half, :] = jnp.where(core[0] == 0, hi, lo)


def partial_hessian(values, image, core, blocks):
    _, width, depth = values.shape
    half = width // (2 * blocks)
    out = jax.ShapeDtypeStruct((width // 2, width), jnp.float32)
    return pl.pallas_call(
        functools.partial(hessian_kernel, blocks, half),
        grid_spec=pltpu.PrefetchScalarGridSpec(
            num_scalar_prefetch=1,
            grid=(3,),
            in_specs=[pl.BlockSpec((1, width, depth), lambda i, t: (i, 0, 0))] * 2,
            out_specs=[pl.BlockSpec(out.shape, lambda i, t: (0, 0))] * 2,
            scratch_shapes=[pltpu.VMEM((width, width), jnp.float32)],
        ),
        out_shape=[out, out],
        compiler_params=pltpu.CompilerParams(vmem_limit_bytes=24 << 20),
        cost_estimate=pl.CostEstimate(
            flops=2 * 3 * width * width * depth, bytes_accessed=12 << 20, transcendentals=0
        ),
        name="partial_hessian",
    )(core, values, image)


def on_device(sensitivity, residual_force, moments, zone_label, misfit):
    cols = sensitivity.shape[1]
    layers = moments.shape[1]
    plane = GX * GY
    n_slab = lax.axis_size("slab")
    n_col = lax.axis_size("col")
    assert n_slab == 2 * n_col
    width = cols * n_col
    me = lax.axis_index("col").astype(jnp.int32)
    slab = lax.axis_index("slab").astype(jnp.int32)
    core, level_z = slab % 2, slab // 2
    lanes = plane // n_col

    firsts, rests = [], []
    for k in range(n_col):
        first, rest = pack(sensitivity, jnp.reshape(me ^ k, (1,)), layers, plane, n_col)
        if k:
            first, rest = exchange(first, "col", k), exchange(rest, "col", k)
        firsts.append(first)
        rests.append(rest)
    buffers = None
    for k in range(n_col):
        top = shifted(firsts[k], "slab", -1)
        place = jnp.stack([me, k ^ me ^ level_z])
        buffers = image_piece(k, place, firsts[k], rests[k], top, moments, buffers, n_col)
    keep, send = partial_hessian(*buffers, jnp.reshape(core, (1,)), n_col)

    mine = keep + exchange(send, "slab", 1)
    parts = [mine[:, k * cols : (k + 1) * cols] for k in range(n_col)]
    mine = parts[0]
    for k in range(1, n_col):
        mine = mine + exchange(parts[k], "col", k)
    half = cols // 2
    parts = [mine[k * half : (k + 1) * half] for k in range(n_col)]
    mine = parts[0]
    for k in range(1, n_col):
        mine = mine + exchange(parts[k], "slab", 2 * k)
    hessian = mine.T

    grad_part = lax.dot_general(
        residual_force,
        sensitivity,
        (((0, 1), (0, 2)), ((), ())),
        preferred_element_type=jnp.float32,
    )
    grad_full = lax.dynamic_update_slice_in_dim(jnp.zeros((width,), jnp.float32), grad_part, me * cols, 0)
    elements = layers * plane
    share = elements // n_col
    offset = me * share
    zone_part = lax.dynamic_slice_in_dim(zone_label.reshape(elements), offset, share, 0)
    misfit_part = lax.dynamic_slice_in_dim(misfit.reshape(elements), offset, share, 0)
    onehot = (zone_part[:, None] == jnp.arange(width, dtype=jnp.int32)[None, :]).astype(jnp.float32)
    zone_part_sum = jnp.dot(misfit_part, onehot, precision=lax.Precision.HIGHEST)
    both = jnp.concatenate([grad_full, zone_part_sum]).reshape(8, -1)
    for axis, count in (("slab", n_slab), ("col", n_col)):
        by = 1
        while by < count:
            both = both + exchange(both, axis, by)
            by *= 2
    both = both.reshape(2, width)
    gradient = both[0]
    zone_misfit = both[1] * (width / (elements * n_slab))
    return (hessian, gradient, zone_misfit)


def solution(mesh):
    in_specs = (
        P(None, "col", "slab"),
        P(None, "slab"),
        P(None, "slab", None),
        P("slab", None),
        P("slab", None),
    )
    out_specs = (P("col", "slab"), P(), P())
    return jax.shard_map(
        on_device, mesh=mesh, in_specs=in_specs, out_specs=out_specs, check_vma=False
    )
```

```python
import functools

import jax
import jax.numpy as jnp
from jax import lax
from jax.experimental import pallas as pl
from jax.experimental.pallas import tpu as pltpu
from jax.sharding import PartitionSpec as P

GX = 64
GY = 16
TILE = 128
EDGE = 256


def exchange(value, axis, by):
    count = lax.axis_size(axis)
    return lax.ppermute(value, axis, [(i, i ^ by) for i in range(count)])


def shifted(value, axis, by):
    count = lax.axis_size(axis)
    pairs = [(i, i + by) for i in range(count) if 0 <= i + by < count]
    return lax.ppermute(value, axis, pairs)


def lane_of(shape):
    return lax.broadcasted_iota(jnp.int32, shape, 1)


def pack_kernel(layers, width, last, target, *refs):
    planes, edges = refs[:layers], refs[layers : 2 * layers]
    first_ref, rest_ref = refs[2 * layers :]
    inside = target[0] != last
    rows = first_ref.shape[0]
    lane = lane_of((rows, TILE))
    for k in range(3):
        first_ref[:, k * width : (k + 1) * width] = planes[0][k]
        for level in range(1, layers):
            start = (3 * (level - 1) + k) * width
            rest_ref[:, start : start + width] = planes[level][k]
    halo = [jnp.zeros((rows, TILE), jnp.float32)] * (EDGE // TILE)
    for k in range(3):
        for level in range(layers):
            tile, at = divmod(edge_at(k, level, layers), TILE)
            edge = edges[level][k].astype(jnp.float32)
            edge = pltpu.roll(edge, at, 1) if at else edge
            halo[tile] = jnp.where((lane >= at) & (lane < at + GY) & inside, edge, halo[tile])
    for tile, value in enumerate(halo):
        start = 3 * width + tile * TILE
        first_ref[:, start : start + TILE] = value.astype(first_ref.dtype)


def edge_at(k, level, layers):
    return (k * (layers + 1) + level) * GY


def pack(sensitivity, target, layers, plane, n_col):
    cols = sensitivity.shape[1]
    width = plane // n_col
    top_block = layers * plane // TILE - 1

    def plane_spec(level):
        return pl.BlockSpec((3, cols, width), lambda i, t: (0, 0, level * n_col + t[0]))

    def edge_spec(level):
        def place(i, t):
            block = (level * plane + (t[0] + 1) * width) // TILE
            return (0, 0, jnp.minimum(block, top_block))

        return pl.BlockSpec((3, cols, TILE), place)

    first = jax.ShapeDtypeStruct((cols, 3 * width + EDGE), sensitivity.dtype)
    rest = jax.ShapeDtypeStruct((cols, 3 * (layers - 1) * width), sensitivity.dtype)
    return pl.pallas_call(
        functools.partial(pack_kernel, layers, width, n_col - 1),
        grid_spec=pltpu.PrefetchScalarGridSpec(
            num_scalar_prefetch=1,
            grid=(1,),
            in_specs=[plane_spec(l) for l in range(layers)] + [edge_spec(l) for l in range(layers)],
            out_specs=[
                pl.BlockSpec(first.shape, lambda i, t: (0, 0)),
                pl.BlockSpec(rest.shape, lambda i, t: (0, 0)),
            ],
        ),
        out_shape=[first, rest],
        compiler_params=pltpu.CompilerParams(vmem_limit_bytes=12 << 20),
        cost_estimate=pl.CostEstimate(flops=0, bytes_accessed=2 << 20, transcendentals=0),
        name="pack",
    )(target, *([sensitivity] * (2 * layers)))


def component(a, b):
    a, b = min(a, b), max(a, b)
    return a if a == b else a + b + 2


def tile_start(k, side, other):
    base = (0, 6, 11)[k]
    return base + (other - k if side == 0 else 3 - k + other)


def build_kernel(layers, width, _, moments_ref, plane_ref, edge_ref, corner_ref, field_ref, ahead_ref):
    f32, bf16 = jnp.float32, jnp.bfloat16
    shape = (GY, width)
    lane = lane_of(shape)
    row = lax.broadcasted_iota(jnp.int32, shape, 0)
    pos_x, pos_y = lane // GY, lane % GY
    same, up, down = row == pos_y, row == pos_y + 1, row == pos_y - 1
    zero = jnp.zeros(shape, f32)
    field_lane = lane_of((8, width))
    columns = width // GY
    near = [pos_x % 3 == r for r in range(3)]
    follow = [(pos_x + 1) % 3 == r for r in range(3)]
    band = [jnp.where((pos_x >= x - 1) & (pos_x <= x + 1), 1.0, 0.0).astype(bf16) for x in range(columns)]
    tile_lane = lane_of((GY, TILE))

    def spread(middle, ahead, behind):
        def whole(value):
            return jnp.broadcast_to(value, shape)

        return jnp.where(same, whole(middle), jnp.where(up, whole(ahead), jnp.where(down, whole(behind), zero)))

    def two_terms(value):
        hi = value.astype(bf16)
        return hi, (value - hi.astype(f32)).astype(bf16)

    edge_ref[...] = jnp.zeros_like(edge_ref)
    field_ref[...] = jnp.zeros_like(field_ref)
    for z in range(layers + 1):
        whole = None
        for level in (z, z - 1):
            if 0 <= level < layers:
                part = moments_ref[:, level, :] * (2.0 / 216.0)
                whole = part if whole is None else whole + part
        field_ref[2 * z, :6] = whole
        if z < layers:
            field_ref[2 * z + 1, :6] = moments_ref[:, z, :] * (1.0 / 216.0)

    for pair in range(2 * layers + 1):
        z, side = divmod(pair, 2)
        element = field_ref[pair]
        before = jnp.where(field_lane >= GY, pltpu.roll(element, GY, 1), 0.0)
        parts = []
        for value in (2.0 * (element + before), element, before):
            lower = jnp.where(field_lane % GY != 0, pltpu.roll(value, 1, 1), 0.0)
            parts.append((2.0 * (value + lower), value, lower))
        for c in range(6):
            here, ahead, behind = [spread(*(v[c : c + 1] for v in part)) for part in parts]
            ahead_ref[pair, c] = ahead[:, width - TILE :]
            scale = 0.5 if side == 0 and c < 3 else None
            spots = []
            for k in range(3):
                for other in range(3):
                    if component(k, other) == c and (side == 1 or other >= k):
                        spots.append(tile_start(k, side, other))
            for r in range(3):
                value = jnp.where(near[r], here, jnp.where(follow[r], ahead, behind))
                if scale is not None:
                    value = value * scale
                for term, piece in enumerate(two_terms(value)):
                    for x in range(r, columns, 3):
                        block = piece * band[x]
                        for spot in spots:
                            start = spot * width + x * GY
                            plane_ref[z, term, start : start + GY, :] = block

    edge_lane = tile_lane // GY == TILE // GY - 1
    for z in range(layers + 1):
        for other_z in range(max(z - 1, 0), min(z + 1, layers) + 1):
            pair = 2 * z if other_z == z else 2 * min(z, other_z) + 1
            for c in range(6):
                value = jnp.where(edge_lane, ahead_ref[pair, c], 0.0)
                for term, piece in enumerate(two_terms(value)):
                    for k in range(3):
                        for other in range(3):
                            if component(k, other) == c:
                                start = edge_at(other, other_z, layers)
                                edge_ref[term, 3 * z + k, start : start + GY, width - TILE :] = piece

    corner_ref[...] = jnp.zeros_like(corner_ref)
    for other_z in range(layers + 1):
        for other in range(3):
            tiles = [jnp.zeros((GY, TILE), f32)] * (EDGE // TILE)
            for z in range(max(other_z - 1, 0), min(other_z + 1, layers) + 1):
                pair = 2 * z if other_z == z else 2 * min(z, other_z) + 1
                for k in range(3):
                    tile, at = divmod(edge_at(k, z, layers), TILE)
                    value = ahead_ref[pair, component(k, other)]
                    turn = (at + GY) % TILE
                    value = pltpu.roll(value, turn, 1) if turn else value
                    tiles[tile] = jnp.where(tile_lane // GY == at // GY, value, tiles[tile])
            start = edge_at(other, other_z, layers)
            for tile, value in enumerate(tiles):
                for term, piece in enumerate(two_terms(value)):
                    corner_ref[term, start : start + GY, tile * TILE : (tile + 1) * TILE] = piece


def build(moments, place, width):
    layers = moments.shape[1]
    shapes = [
        jax.ShapeDtypeStruct((layers + 1, 2, 15 * width, width), jnp.bfloat16),
        jax.ShapeDtypeStruct((2, 3 * (layers + 1), EDGE, width), jnp.bfloat16),
        jax.ShapeDtypeStruct((2, EDGE, EDGE), jnp.bfloat16),
    ]
    return pl.pallas_call(
        functools.partial(build_kernel, layers, width),
        grid_spec=pltpu.PrefetchScalarGridSpec(
            num_scalar_prefetch=1,
            grid=(1,),
            in_specs=[pl.BlockSpec((6, layers, width), lambda i, t: (0, 0, t[0]))],
            out_specs=[pl.BlockSpec(memory_space=pltpu.VMEM)] * 3,
            scratch_shapes=[
                pltpu.VMEM((2 * layers + 1, 8, width), jnp.float32),
                pltpu.VMEM((2 * layers + 1, 6, GY, TILE), jnp.float32),
            ],
        ),
        out_shape=shapes,
        compiler_params=pltpu.CompilerParams(vmem_limit_bytes=32 << 20),
        cost_estimate=pl.CostEstimate(flops=20 << 20, bytes_accessed=24 << 20, transcendentals=0),
        name="build",
    )(place, moments)


def image_kernel(layers, width, first_ref, rest_ref, top_ref, plane_ref, edge_ref, corner_ref, *refs):
    values_ref, image_ref = refs[-2:]
    f32, bf16 = jnp.float32, jnp.bfloat16
    depth = 3 * (layers + 1) * width
    rows = first_ref.shape[0]
    values_ref[:, : 3 * width] = first_ref[:, : 3 * width]
    values_ref[:, 3 * width : 3 * layers * width] = rest_ref[...]
    values_ref[:, 3 * layers * width : depth] = top_ref[:, : 3 * width]
    lane = lane_of((rows, EDGE))
    group = lane // GY
    halo = first_ref[:, 3 * width :].astype(f32)
    top = pltpu.roll(top_ref[:, 3 * width :].astype(f32), layers * GY, 1)
    halo = jnp.where(group % (layers + 1) == layers, top, halo)
    halo = jnp.where(group < 3 * (layers + 1), halo, 0.0).astype(bf16)
    values_ref[:, depth:] = halo

    def dot(a, b):
        return jnp.dot(a, b, preferred_element_type=f32)

    for z in range(layers + 1):
        for k in range(3):
            lo = (3 * z + k) * width
            hi = min(3 * (z + 2) * width, depth)
            value = values_ref[:, lo:hi]
            start = tile_start(k, 0, k) * width
            total = dot(halo, edge_ref[0, 3 * z + k]) + dot(halo, edge_ref[1, 3 * z + k])
            for term in range(2):
                total = total + dot(value, plane_ref[z, term, start : start + hi - lo, :])
            image_ref[:, lo : lo + width] = total.astype(bf16)
    image_ref[:, depth:] = (dot(halo, corner_ref[0]) + dot(halo, corner_ref[1])).astype(bf16)


def image_piece(index, first, rest, top, matrix, buffers, n_col):
    cols = first.shape[0]
    width = (first.shape[1] - EDGE) // 3
    layers = rest.shape[1] // (3 * width) + 1
    total = 3 * (layers + 1) * width + EDGE
    shape = jax.ShapeDtypeStruct((cols * n_col, total), first.dtype)
    in_specs = [pl.BlockSpec(x.shape, lambda i: (0, 0)) for x in (first, rest, top)]
    in_specs += [pl.BlockSpec(memory_space=pltpu.VMEM)] * 3
    args = [first, rest, top, *matrix]
    aliases = {}
    if buffers is not None:
        in_specs += [pl.BlockSpec(memory_space=pl.ANY)] * 2
        args += list(buffers)
        aliases = {6: 0, 7: 1}
    return pl.pallas_call(
        functools.partial(image_kernel, layers, width),
        grid=(1,),
        in_specs=in_specs,
        out_specs=[pl.BlockSpec((cols, total), lambda i: (index, 0))] * 2,
        out_shape=[shape, shape],
        input_output_aliases=aliases,
        compiler_params=pltpu.CompilerParams(vmem_limit_bytes=40 << 20),
        cost_estimate=pl.CostEstimate(
            flops=2 * 164 * cols * width * width, bytes_accessed=4 << 20, transcendentals=0
        ),
        name="image",
    )(*args)


def hessian_kernel(blocks, half, place, values_ref, image_ref, keep_ref, send_ref, total):
    step = pl.program_id(0)

    @pl.when(step == 0)
    def _():
        total[...] = jnp.zeros_like(total)

    total[...] += lax.dot_general(
        values_ref[...], image_ref[...], (((1,), (1,)), ((), ())), preferred_element_type=jnp.float32
    )

    @pl.when(step == pl.num_programs(0) - 1)
    def _():
        full = total[...] + total[...].T
        for b in range(blocks):
            lo = full[2 * b * half : (2 * b + 1) * half, :]
            hi = full[(2 * b + 1) * half : (2 * b + 2) * half, :]
            rows = pl.ds(pl.multiple_of((b ^ place[1]) * half, half), half)
            keep_ref[rows, :] = jnp.where(place[0] == 0, lo, hi)
            send_ref[rows, :] = jnp.where(place[0] == 0, hi, lo)


def partial_hessian(values, image, place, blocks):
    width, depth = values.shape
    half = width // (2 * blocks)
    steps = 4 if depth % (4 * TILE) == 0 else 1
    out = jax.ShapeDtypeStruct((width // 2, width), jnp.float32)
    return pl.pallas_call(
        functools.partial(hessian_kernel, blocks, half),
        grid_spec=pltpu.PrefetchScalarGridSpec(
            num_scalar_prefetch=1,
            grid=(steps,),
            in_specs=[pl.BlockSpec((width, depth // steps), lambda i, t: (0, i))] * 2,
            out_specs=[pl.BlockSpec(out.shape, lambda i, t: (0, 0))] * 2,
            scratch_shapes=[pltpu.VMEM((width, width), jnp.float32)],
        ),
        out_shape=[out, out],
        compiler_params=pltpu.CompilerParams(vmem_limit_bytes=24 << 20),
        cost_estimate=pl.CostEstimate(
            flops=2 * width * width * depth, bytes_accessed=12 << 20, transcendentals=0
        ),
        name="partial_hessian",
    )(place, values, image)


def small_sums(sensitivity, residual_force, zone_label, misfit, me, n_col, width):
    cols = sensitivity.shape[1]
    grad_part = lax.dot_general(
        residual_force,
        sensitivity,
        (((0, 1), (0, 2)), ((), ())),
        preferred_element_type=jnp.float32,
    )
    grad_full = lax.dynamic_update_slice_in_dim(jnp.zeros((width,), jnp.float32), grad_part, me * cols, 0)
    elements = zone_label.size
    share = elements // n_col
    offset = me * share
    zone_part = lax.dynamic_slice_in_dim(zone_label.reshape(elements), offset, share, 0)
    misfit_part = lax.dynamic_slice_in_dim(misfit.reshape(elements), offset, share, 0)
    onehot = (zone_part[:, None] == jnp.arange(width, dtype=jnp.int32)[None, :]).astype(jnp.float32)
    zone_part_sum = jnp.dot(misfit_part, onehot, precision=lax.Precision.HIGHEST)
    return jnp.concatenate([grad_full, zone_part_sum]).reshape(8, -1)


def on_device(sensitivity, residual_force, moments, zone_label, misfit):
    cols = sensitivity.shape[1]
    layers = moments.shape[1]
    plane = GX * GY
    n_slab = lax.axis_size("slab")
    n_col = lax.axis_size("col")
    assert n_slab == 2 * n_col
    width = cols * n_col
    me = lax.axis_index("col").astype(jnp.int32)
    slab = lax.axis_index("slab").astype(jnp.int32)
    core, level_z = slab % 2, slab // 2

    firsts, rests = [], []
    for k in range(n_col):
        first, rest = pack(sensitivity, jnp.reshape(me ^ k, (1,)), layers, plane, n_col)
        if k:
            first, rest = exchange(first, "col", k), exchange(rest, "col", k)
        firsts.append(first)
        rests.append(rest)

    both = small_sums(sensitivity, residual_force, zone_label, misfit, me, n_col, width)
    stages = []
    for axis, count in (("slab", n_slab), ("col", n_col)):
        stages += [(axis, 1 << b) for b in range(count.bit_length() - 1)]
    matrix = build(moments, jnp.reshape(me, (1,)), plane // n_col)
    buffers = None
    for k in range(n_col):
        top = shifted(firsts[k], "slab", -1)
        for axis, by in stages[2 * k : 2 * k + 2]:
            both = both + exchange(both, axis, by)
        both, top = lax.optimization_barrier((both, top))
        buffers = image_piece(k, firsts[k], rests[k], top, matrix, buffers, n_col)
    place = jnp.stack([core, me ^ level_z])
    keep, send = partial_hessian(*buffers, place, n_col)

    mine = keep + exchange(send, "slab", 1)
    parts = [mine[:, k * cols : (k + 1) * cols] for k in range(n_col)]
    mine = parts[0]
    for k in range(1, n_col):
        mine = mine + exchange(parts[k], "col", k)
    half = cols // 2
    parts = [mine[k * half : (k + 1) * half] for k in range(n_col)]
    mine = parts[0]
    for k in range(1, n_col):
        mine = mine + exchange(parts[k], "slab", 2 * k)
    hessian = mine.T

    both = both.reshape(2, width)
    gradient = both[0]
    zone_misfit = both[1] * (width / (layers * plane * n_slab))
    return (hessian, gradient, zone_misfit)


def solution(mesh):
    in_specs = (
        P(None, "col", "slab"),
        P(None, "slab"),
        P(None, "slab", None),
        P("slab", None),
        P("slab", None),
    )
    out_specs = (P("col", "slab"), P(), P())
    return jax.shard_map(
        on_device, mesh=mesh, in_specs=in_specs, out_specs=out_specs, check_vma=False
    )
```

```python
import functools

import jax
import jax.numpy as jnp
from jax import lax
from jax.experimental import pallas as pl
from jax.experimental.pallas import tpu as pltpu
from jax.sharding import PartitionSpec as P

GX = 64
GY = 16
TILE = 128
EDGE = 256


def exchange(value, axis, by):
    count = lax.axis_size(axis)
    return lax.ppermute(value, axis, [(i, i ^ by) for i in range(count)])


def shifted(value, axis, by):
    count = lax.axis_size(axis)
    pairs = [(i, i + by) for i in range(count) if 0 <= i + by < count]
    return lax.ppermute(value, axis, pairs)


def lane_of(shape):
    return lax.broadcasted_iota(jnp.int32, shape, 1)


def pack_kernel(layers, width, last, target, *refs):
    planes, edges = refs[:layers], refs[layers : 2 * layers]
    first_ref, rest_ref = refs[2 * layers], refs[-1]
    offset = 0 if rest_ref is not first_ref else 3 * width + EDGE
    inside = target[0] != last
    rows = first_ref.shape[0]
    lane = lane_of((rows, TILE))
    for k in range(3):
        first_ref[:, k * width : (k + 1) * width] = planes[0][k]
        for level in range(1, layers):
            start = offset + (3 * (level - 1) + k) * width
            rest_ref[:, start : start + width] = planes[level][k]
    halo = [jnp.zeros((rows, TILE), jnp.float32)] * (EDGE // TILE)
    for k in range(3):
        for level in range(layers):
            tile, at = divmod(edge_at(k, level, layers), TILE)
            edge = edges[level][k].astype(jnp.float32)
            edge = pltpu.roll(edge, at, 1) if at else edge
            halo[tile] = jnp.where((lane >= at) & (lane < at + GY) & inside, edge, halo[tile])
    for tile, value in enumerate(halo):
        start = 3 * width + tile * TILE
        first_ref[:, start : start + TILE] = value.astype(first_ref.dtype)


def edge_at(k, level, layers):
    return (k * (layers + 1) + level) * GY


def pack(sensitivity, target, layers, plane, n_col, split):
    cols = sensitivity.shape[1]
    width = plane // n_col
    top_block = layers * plane // TILE - 1

    def plane_spec(level):
        return pl.BlockSpec((3, cols, width), lambda i, t: (0, 0, level * n_col + t[0]))

    def edge_spec(level):
        def place(i, t):
            block = (level * plane + (t[0] + 1) * width) // TILE
            return (0, 0, jnp.minimum(block, top_block))

        return pl.BlockSpec((3, cols, TILE), place)

    sizes = [3 * width + EDGE, 3 * (layers - 1) * width]
    outs = [jax.ShapeDtypeStruct((cols, size), sensitivity.dtype) for size in (sizes if split else [sum(sizes)])]
    return pl.pallas_call(
        functools.partial(pack_kernel, layers, width, n_col - 1),
        grid_spec=pltpu.PrefetchScalarGridSpec(
            num_scalar_prefetch=1,
            grid=(1,),
            in_specs=[plane_spec(l) for l in range(layers)] + [edge_spec(l) for l in range(layers)],
            out_specs=[pl.BlockSpec(out.shape, lambda i, t: (0, 0)) for out in outs],
        ),
        out_shape=outs,
        compiler_params=pltpu.CompilerParams(vmem_limit_bytes=12 << 20),
        cost_estimate=pl.CostEstimate(flops=0, bytes_accessed=2 << 20, transcendentals=0),
        name="pack",
    )(target, *([sensitivity] * (2 * layers)))


def component(a, b):
    a, b = min(a, b), max(a, b)
    return a if a == b else a + b + 2


def tile_start(k, side, other):
    base = (0, 6, 11)[k]
    return base + (other - k if side == 0 else 3 - k + other)


def build_kernel(layers, width, _, moments_ref, plane_ref, edge_ref, corner_ref, field_ref, ahead_ref):
    f32, bf16 = jnp.float32, jnp.bfloat16
    shape = (GY, width)
    lane = lane_of(shape)
    row = lax.broadcasted_iota(jnp.int32, shape, 0)
    pos_x, pos_y = lane // GY, lane % GY
    same, up, down = row == pos_y, row == pos_y + 1, row == pos_y - 1
    zero = jnp.zeros(shape, f32)
    field_lane = lane_of((8, width))
    columns = width // GY
    near = [pos_x % 3 == r for r in range(3)]
    follow = [(pos_x + 1) % 3 == r for r in range(3)]
    band = [jnp.where((pos_x >= x - 1) & (pos_x <= x + 1), 1.0, 0.0).astype(bf16) for x in range(columns)]
    tile_lane = lane_of((GY, TILE))

    def spread(middle, ahead, behind):
        def whole(value):
            return jnp.broadcast_to(value, shape)

        return jnp.where(same, whole(middle), jnp.where(up, whole(ahead), jnp.where(down, whole(behind), zero)))

    def two_terms(value):
        hi = value.astype(bf16)
        return hi, (value - hi.astype(f32)).astype(bf16)

    edge_ref[...] = jnp.zeros_like(edge_ref)
    field_ref[...] = jnp.zeros_like(field_ref)
    for z in range(layers + 1):
        whole = None
        for level in (z, z - 1):
            if 0 <= level < layers:
                part = moments_ref[:, level, :] * (2.0 / 216.0)
                whole = part if whole is None else whole + part
        field_ref[2 * z, :6] = whole
        if z < layers:
            field_ref[2 * z + 1, :6] = moments_ref[:, z, :] * (1.0 / 216.0)

    for pair in range(2 * layers + 1):
        z, side = divmod(pair, 2)
        element = field_ref[pair]
        before = jnp.where(field_lane >= GY, pltpu.roll(element, GY, 1), 0.0)
        parts = []
        for value in (2.0 * (element + before), element, before):
            lower = jnp.where(field_lane % GY != 0, pltpu.roll(value, 1, 1), 0.0)
            parts.append((2.0 * (value + lower), value, lower))
        for c in range(6):
            here, ahead, behind = [spread(*(v[c : c + 1] for v in part)) for part in parts]
            ahead_ref[pair, c] = ahead[:, width - TILE :]
            scale = 0.5 if side == 0 and c < 3 else None
            spots = []
            for k in range(3):
                for other in range(3):
                    if component(k, other) == c and (side == 1 or other >= k):
                        spots.append(tile_start(k, side, other))
            for r in range(3):
                value = jnp.where(near[r], here, jnp.where(follow[r], ahead, behind))
                if scale is not None:
                    value = value * scale
                for term, piece in enumerate(two_terms(value)):
                    for x in range(r, columns, 3):
                        block = piece * band[x]
                        for spot in spots:
                            start = spot * width + x * GY
                            plane_ref[z, term, start : start + GY, :] = block

    edge_lane = tile_lane // GY == TILE // GY - 1
    for z in range(layers + 1):
        for other_z in range(max(z - 1, 0), min(z + 1, layers) + 1):
            pair = 2 * z if other_z == z else 2 * min(z, other_z) + 1
            for c in range(6):
                value = jnp.where(edge_lane, ahead_ref[pair, c], 0.0)
                for term, piece in enumerate(two_terms(value)):
                    for k in range(3):
                        for other in range(3):
                            if component(k, other) == c:
                                start = edge_at(other, other_z, layers)
                                edge_ref[term, 3 * z + k, start : start + GY, width - TILE :] = piece

    corner_ref[...] = jnp.zeros_like(corner_ref)
    for other_z in range(layers + 1):
        for other in range(3):
            tiles = [jnp.zeros((GY, TILE), f32)] * (EDGE // TILE)
            for z in range(max(other_z - 1, 0), min(other_z + 1, layers) + 1):
                pair = 2 * z if other_z == z else 2 * min(z, other_z) + 1
                for k in range(3):
                    tile, at = divmod(edge_at(k, z, layers), TILE)
                    value = ahead_ref[pair, component(k, other)]
                    turn = (at + GY) % TILE
                    value = pltpu.roll(value, turn, 1) if turn else value
                    tiles[tile] = jnp.where(tile_lane // GY == at // GY, value, tiles[tile])
            start = edge_at(other, other_z, layers)
            for tile, value in enumerate(tiles):
                for term, piece in enumerate(two_terms(value)):
                    corner_ref[term, start : start + GY, tile * TILE : (tile + 1) * TILE] = piece


def in_vmem(x):
    return pltpu.with_memory_space_constraint(x, pltpu.VMEM)


def build(moments, place, width):
    layers = moments.shape[1]
    shapes = [
        pltpu.VMEM((layers + 1, 2, 15 * width, width), jnp.bfloat16),
        pltpu.VMEM((2, 3 * (layers + 1), EDGE, width), jnp.bfloat16),
        pltpu.VMEM((2, EDGE, EDGE), jnp.bfloat16),
    ]
    out = pl.pallas_call(
        functools.partial(build_kernel, layers, width),
        grid_spec=pltpu.PrefetchScalarGridSpec(
            num_scalar_prefetch=1,
            grid=(1,),
            in_specs=[pl.BlockSpec((6, layers, width), lambda i, t: (0, 0, t[0]))],
            out_specs=[pl.BlockSpec(memory_space=pltpu.VMEM)] * 3,
            scratch_shapes=[
                pltpu.VMEM((2 * layers + 1, 8, width), jnp.float32),
                pltpu.VMEM((2 * layers + 1, 6, GY, TILE), jnp.float32),
            ],
        ),
        out_shape=shapes,
        compiler_params=pltpu.CompilerParams(vmem_limit_bytes=6 << 20),
        cost_estimate=pl.CostEstimate(flops=20 << 20, bytes_accessed=24 << 20, transcendentals=0),
        name="build",
    )(place, moments)
    return [in_vmem(x) for x in out]


def image_kernel(layers, width, parts, index, blocks, *refs):
    refs = list(refs)
    pieces = [refs.pop(0) for _ in range(parts)]
    first_ref, rest_ref = pieces[0], pieces[-1]
    offset = 0 if parts == 2 else 3 * width + EDGE
    top_ref, plane_ref, edge_ref, corner_ref = (refs.pop(0) for _ in range(4))
    before = [(refs.pop(0), refs.pop(0)) for _ in range(index)]
    last = index == blocks - 1
    if last:
        block_refs = [refs.pop(0) for _ in range(index)]
        place = refs.pop(0)
        keep_ref, send_ref, values_ref, image_ref = refs
    else:
        values_ref, image_ref, block_ref = refs
    f32, bf16 = jnp.float32, jnp.bfloat16
    depth = 3 * (layers + 1) * width
    rows = first_ref.shape[0]
    values_ref[:, : 3 * width] = first_ref[:, : 3 * width]
    values_ref[:, 3 * width : 3 * layers * width] = rest_ref[:, offset:]
    values_ref[:, 3 * layers * width : depth] = top_ref[:, : 3 * width]
    lane = lane_of((rows, EDGE))
    group = lane // GY
    halo = first_ref[:, 3 * width : 3 * width + EDGE].astype(f32)
    top = pltpu.roll(top_ref[:, 3 * width :].astype(f32), layers * GY, 1)
    halo = jnp.where(group % (layers + 1) == layers, top, halo)
    halo = jnp.where(group < 3 * (layers + 1), halo, 0.0).astype(bf16)
    values_ref[:, depth:] = halo

    def dot(a, b):
        return jnp.dot(a, b, preferred_element_type=f32)

    for z in range(layers + 1):
        for k in range(3):
            lo = (3 * z + k) * width
            hi = min(3 * (z + 2) * width, depth)
            value = values_ref[:, lo:hi]
            start = tile_start(k, 0, k) * width
            total = dot(halo, edge_ref[0, 3 * z + k]) + dot(halo, edge_ref[1, 3 * z + k])
            for term in range(2):
                total = total + dot(value, plane_ref[z, term, start : start + hi - lo, :])
            image_ref[:, lo : lo + width] = total.astype(bf16)
    image_ref[:, depth:] = (dot(halo, corner_ref[0]) + dot(halo, corner_ref[1])).astype(bf16)

    def product(a, b):
        return lax.dot_general(a[...], b[...], (((1,), (1,)), ((), ())), preferred_element_type=f32)

    found = [product(v, image_ref) + product(i, values_ref) for v, i in before]
    own = product(values_ref, image_ref)
    found.append(own + own.T)
    if not last:
        for j, value in enumerate(found):
            block_ref[j] = value
        return
    half = rows // 2
    for i in range(blocks):
        at = pl.ds(pl.multiple_of((i ^ place[1]) * half, half), half)
        for j in range(blocks):
            lo, hi = min(i, j), max(i, j)
            block = found[lo] if hi == index else block_refs[hi][lo]
            block = block.T if i > j else block
            for ref, low in ((keep_ref, 0), (send_ref, 1)):
                ref[at, j * rows : (j + 1) * rows] = jnp.where(place[0] == low, block[:half], block[half:])


def image_piece(index, piece, top, matrix, before, blocks, place, n_col):
    cols = top.shape[0]
    width = (top.shape[1] - EDGE) // 3
    layers = (sum(x.shape[1] for x in piece) - EDGE) // (3 * width)
    total = 3 * (layers + 1) * width + EDGE
    args = [*piece, top, *matrix, *(x for pair in before for x in pair)]
    shape = pltpu.VMEM((cols, total), top.dtype)
    scratch = []
    vmem = pl.BlockSpec(memory_space=pltpu.VMEM)
    in_specs = [vmem] * len(args)
    if index == n_col - 1:
        args += [*blocks, place]
        in_specs += [vmem] * len(blocks) + [pl.BlockSpec(memory_space=pltpu.SMEM)]
        outs = [pltpu.VMEM((cols * n_col // 2, cols * n_col), jnp.float32)] * 2
        scratch = [shape] * 2
    else:
        outs = [shape, shape, pltpu.VMEM((index + 1, cols, cols), jnp.float32)]
    flops = 2 * 164 * cols * width * width + 4 * (index + 1) * cols * cols * total
    out = pl.pallas_call(
        functools.partial(image_kernel, layers, width, len(piece), index, n_col),
        in_specs=in_specs,
        out_specs=[vmem] * len(outs),
        out_shape=outs,
        scratch_shapes=scratch,
        compiler_params=pltpu.CompilerParams(vmem_limit_bytes=8 << 20),
        cost_estimate=pl.CostEstimate(flops=flops, bytes_accessed=24 << 20, transcendentals=0),
        name="image",
    )(*args)
    return out if index == n_col - 1 else [in_vmem(x) for x in out]


def small_sums(sensitivity, residual_force, zone_label, misfit, me, n_col, width):
    cols = sensitivity.shape[1]
    grad_part = lax.dot_general(
        residual_force,
        sensitivity,
        (((0, 1), (0, 2)), ((), ())),
        preferred_element_type=jnp.float32,
    )
    grad_full = lax.dynamic_update_slice_in_dim(jnp.zeros((width,), jnp.float32), grad_part, me * cols, 0)
    elements = zone_label.size
    share = elements // n_col
    offset = me * share
    zone_part = lax.dynamic_slice_in_dim(zone_label.reshape(elements), offset, share, 0)
    misfit_part = lax.dynamic_slice_in_dim(misfit.reshape(elements), offset, share, 0)
    onehot = (zone_part[:, None] == jnp.arange(width, dtype=jnp.int32)[None, :]).astype(jnp.float32)
    zone_part_sum = jnp.dot(misfit_part, onehot, precision=lax.Precision.HIGHEST)
    return jnp.concatenate([grad_full, zone_part_sum]).reshape(8, -1)


def on_device(sensitivity, residual_force, moments, zone_label, misfit):
    cols = sensitivity.shape[1]
    layers = moments.shape[1]
    plane = GX * GY
    n_slab = lax.axis_size("slab")
    n_col = lax.axis_size("col")
    assert n_slab == 2 * n_col
    width = cols * n_col
    me = lax.axis_index("col").astype(jnp.int32)
    slab = lax.axis_index("slab").astype(jnp.int32)
    core, level_z = slab % 2, slab // 2

    source = pltpu.with_memory_space_constraint(sensitivity, pltpu.HBM)
    bottom = 3 * (plane // n_col) + EDGE
    pieces = [None] * n_col
    for k in (*range(1, n_col), 0):
        packed = pack(source, jnp.reshape(me ^ k, (1,)), layers, plane, n_col, k == n_col - 1)
        pieces[k] = [exchange(x, "col", k) if k else x for x in packed]
    both = small_sums(sensitivity, residual_force, zone_label, misfit, me, n_col, width)
    stages = []
    for axis, count in (("slab", n_slab), ("col", n_col)):
        stages += [(axis, 1 << b) for b in range(count.bit_length() - 1)]
    matrix = build(moments, jnp.reshape(me, (1,)), plane // n_col)
    place = jnp.stack([core, me ^ level_z])
    before, blocks = [], []
    for k in range(n_col):
        top = shifted(pieces[k][0][:, :bottom], "slab", -1)
        for axis, by in stages[k :: n_col]:
            both = both + exchange(both, axis, by)
        both, top = lax.optimization_barrier((both, top))
        out = image_piece(k, pieces[k], top, matrix, before, blocks, place, n_col)
        if k < n_col - 1:
            before.append(out[:2])
            blocks.append(out[2])
    keep, send = out

    mine = keep + exchange(send, "slab", 1)
    parts = [mine[:, k * cols : (k + 1) * cols] for k in range(n_col)]
    mine = parts[0]
    for k in range(1, n_col):
        mine = mine + exchange(parts[k], "col", k)
    half = cols // 2
    parts = [mine[k * half : (k + 1) * half] for k in range(n_col)]
    mine = parts[0]
    for k in range(1, n_col):
        mine = mine + exchange(parts[k], "slab", 2 * k)
    hessian = mine.T

    both = both.reshape(2, width)
    gradient = both[0]
    zone_misfit = both[1] * (width / (layers * plane * n_slab))
    return (hessian, gradient, zone_misfit)


def solution(mesh):
    in_specs = (
        P(None, "col", "slab"),
        P(None, "slab"),
        P(None, "slab", None),
        P("slab", None),
        P("slab", None),
    )
    out_specs = (P("col", "slab"), P(), P())
    return jax.shard_map(
        on_device, mesh=mesh, in_specs=in_specs, out_specs=out_specs, check_vma=False
    )
```

```python
import functools

import jax
import jax.numpy as jnp
from jax import lax
from jax.experimental import pallas as pl
from jax.experimental.pallas import tpu as pltpu
from jax.sharding import PartitionSpec as P

GX = 64
GY = 16
TILE = 128
EDGE = 256


def exchange(value, axis, by):
    count = lax.axis_size(axis)
    return lax.ppermute(value, axis, [(i, i ^ by) for i in range(count)])


def shifted(value, axis, by):
    count = lax.axis_size(axis)
    pairs = [(i, i + by) for i in range(count) if 0 <= i + by < count]
    return lax.ppermute(value, axis, pairs)


def lane_of(shape):
    return lax.broadcasted_iota(jnp.int32, shape, 1)


def pack_kernel(layers, width, last, turn, target, *refs):
    planes, edges = refs[:layers], refs[layers : 2 * layers]
    first_ref, rest_ref, next_ref = refs[2 * layers], refs[-2], refs[-1]
    next_ref[0] = target[0] ^ turn
    offset = 0 if rest_ref is not first_ref else 3 * width + EDGE
    inside = target[0] != last
    rows = first_ref.shape[0]
    lane = lane_of((rows, TILE))
    for k in range(3):
        first_ref[:, k * width : (k + 1) * width] = planes[0][k]
        for level in range(1, layers):
            start = offset + (3 * (level - 1) + k) * width
            rest_ref[:, start : start + width] = planes[level][k]
    halo = [jnp.zeros((rows, TILE), jnp.float32)] * (EDGE // TILE)
    for k in range(3):
        for level in range(layers):
            tile, at = divmod(edge_at(k, level, layers), TILE)
            edge = edges[level][k].astype(jnp.float32)
            edge = pltpu.roll(edge, at, 1) if at else edge
            halo[tile] = jnp.where((lane >= at) & (lane < at + GY) & inside, edge, halo[tile])
    for tile, value in enumerate(halo):
        start = 3 * width + tile * TILE
        first_ref[:, start : start + TILE] = value.astype(first_ref.dtype)


def edge_at(k, level, layers):
    return (k * (layers + 1) + level) * GY


def pack(sensitivity, target, turn, layers, plane, n_col, split):
    cols = sensitivity.shape[1]
    width = plane // n_col
    top_block = layers * plane // TILE - 1

    def plane_spec(level):
        return pl.BlockSpec((3, cols, width), lambda i, t: (0, 0, level * n_col + t[0]))

    def edge_spec(level):
        def place(i, t):
            block = (level * plane + (t[0] + 1) * width) // TILE
            return (0, 0, jnp.minimum(block, top_block))

        return pl.BlockSpec((3, cols, TILE), place)

    sizes = [3 * width + EDGE, 3 * (layers - 1) * width]
    outs = [jax.ShapeDtypeStruct((cols, size), sensitivity.dtype) for size in (sizes if split else [sum(sizes)])]
    return pl.pallas_call(
        functools.partial(pack_kernel, layers, width, n_col - 1, turn),
        grid_spec=pltpu.PrefetchScalarGridSpec(
            num_scalar_prefetch=1,
            grid=(1,),
            in_specs=[plane_spec(l) for l in range(layers)] + [edge_spec(l) for l in range(layers)],
            out_specs=[pl.BlockSpec(out.shape, lambda i, t: (0, 0)) for out in outs]
            + [pl.BlockSpec(memory_space=pltpu.SMEM)],
        ),
        out_shape=[*outs, jax.ShapeDtypeStruct((1,), jnp.int32)],
        compiler_params=pltpu.CompilerParams(vmem_limit_bytes=12 << 20),
        cost_estimate=pl.CostEstimate(flops=0, bytes_accessed=2 << 20, transcendentals=0),
        name="pack",
    )(target, *([sensitivity] * (2 * layers)))


def crop_kernel(piece_ref, _, out_ref):
    out_ref[...] = piece_ref[:, : out_ref.shape[1]]


def crop(piece, size, after):
    return pl.pallas_call(
        crop_kernel,
        in_specs=[pl.BlockSpec(memory_space=pltpu.VMEM), pl.BlockSpec(memory_space=pl.ANY)],
        out_specs=pl.BlockSpec(memory_space=pltpu.VMEM),
        out_shape=jax.ShapeDtypeStruct((piece.shape[0], size), piece.dtype),
        compiler_params=pltpu.CompilerParams(vmem_limit_bytes=4 << 20),
        cost_estimate=pl.CostEstimate(flops=0, bytes_accessed=1 << 19, transcendentals=0),
        name="crop",
    )(piece, after)


def component(a, b):
    a, b = min(a, b), max(a, b)
    return a if a == b else a + b + 2


def tile_start(k, side, other):
    base = (0, 6, 11)[k]
    return base + (other - k if side == 0 else 3 - k + other)


def build_kernel(layers, width, _, moments_ref, plane_ref, edge_ref, corner_ref, field_ref, ahead_ref):
    f32, bf16 = jnp.float32, jnp.bfloat16
    shape = (GY, width)
    lane = lane_of(shape)
    row = lax.broadcasted_iota(jnp.int32, shape, 0)
    pos_x, pos_y = lane // GY, lane % GY
    same, up, down = row == pos_y, row == pos_y + 1, row == pos_y - 1
    zero = jnp.zeros(shape, f32)
    field_lane = lane_of((8, width))
    columns = width // GY
    near = [pos_x % 3 == r for r in range(3)]
    follow = [(pos_x + 1) % 3 == r for r in range(3)]
    band = [jnp.where((pos_x >= x - 1) & (pos_x <= x + 1), 1.0, 0.0).astype(bf16) for x in range(columns)]
    tile_lane = lane_of((GY, TILE))

    def spread(middle, ahead, behind):
        def whole(value):
            return jnp.broadcast_to(value, shape)

        return jnp.where(same, whole(middle), jnp.where(up, whole(ahead), jnp.where(down, whole(behind), zero)))

    def two_terms(value):
        hi = value.astype(bf16)
        return hi, (value - hi.astype(f32)).astype(bf16)

    edge_ref[...] = jnp.zeros_like(edge_ref)
    field_ref[...] = jnp.zeros_like(field_ref)
    for z in range(layers + 1):
        whole = None
        for level in (z, z - 1):
            if 0 <= level < layers:
                part = moments_ref[:, level, :] * (2.0 / 216.0)
                whole = part if whole is None else whole + part
        field_ref[2 * z, :6] = whole
        if z < layers:
            field_ref[2 * z + 1, :6] = moments_ref[:, z, :] * (1.0 / 216.0)

    for pair in range(2 * layers + 1):
        z, side = divmod(pair, 2)
        element = field_ref[pair]
        before = jnp.where(field_lane >= GY, pltpu.roll(element, GY, 1), 0.0)
        parts = []
        for value in (2.0 * (element + before), element, before):
            lower = jnp.where(field_lane % GY != 0, pltpu.roll(value, 1, 1), 0.0)
            parts.append((2.0 * (value + lower), value, lower))
        for c in range(6):
            here, ahead, behind = [spread(*(v[c : c + 1] for v in part)) for part in parts]
            ahead_ref[pair, c] = ahead[:, width - TILE :]
            scale = 0.5 if side == 0 and c < 3 else None
            spots = []
            for k in range(3):
                for other in range(3):
                    if component(k, other) == c and (side == 1 or other >= k):
                        spots.append(tile_start(k, side, other))
            for r in range(3):
                value = jnp.where(near[r], here, jnp.where(follow[r], ahead, behind))
                if scale is not None:
                    value = value * scale
                for term, piece in enumerate(two_terms(value)):
                    for x in range(r, columns, 3):
                        block = piece * band[x]
                        for spot in spots:
                            start = spot * width + x * GY
                            plane_ref[z, term, start : start + GY, :] = block

    edge_lane = tile_lane // GY == TILE // GY - 1
    for z in range(layers + 1):
        for other_z in range(max(z - 1, 0), min(z + 1, layers) + 1):
            pair = 2 * z if other_z == z else 2 * min(z, other_z) + 1
            for c in range(6):
                value = jnp.where(edge_lane, ahead_ref[pair, c], 0.0)
                for term, piece in enumerate(two_terms(value)):
                    for k in range(3):
                        for other in range(3):
                            if component(k, other) == c:
                                start = edge_at(other, other_z, layers)
                                edge_ref[term, 3 * z + k, start : start + GY, width - TILE :] = piece

    corner_ref[...] = jnp.zeros_like(corner_ref)
    for other_z in range(layers + 1):
        for other in range(3):
            tiles = [jnp.zeros((GY, TILE), f32)] * (EDGE // TILE)
            for z in range(max(other_z - 1, 0), min(other_z + 1, layers) + 1):
                pair = 2 * z if other_z == z else 2 * min(z, other_z) + 1
                for k in range(3):
                    tile, at = divmod(edge_at(k, z, layers), TILE)
                    value = ahead_ref[pair, component(k, other)]
                    turn = (at + GY) % TILE
                    value = pltpu.roll(value, turn, 1) if turn else value
                    tiles[tile] = jnp.where(tile_lane // GY == at // GY, value, tiles[tile])
            start = edge_at(other, other_z, layers)
            for tile, value in enumerate(tiles):
                for term, piece in enumerate(two_terms(value)):
                    corner_ref[term, start : start + GY, tile * TILE : (tile + 1) * TILE] = piece


def in_vmem(x):
    return pltpu.with_memory_space_constraint(x, pltpu.VMEM)


def build(moments, place, width):
    layers = moments.shape[1]
    shapes = [
        pltpu.VMEM((layers + 1, 2, 15 * width, width), jnp.bfloat16),
        pltpu.VMEM((2, 3 * (layers + 1), EDGE, width), jnp.bfloat16),
        pltpu.VMEM((2, EDGE, EDGE), jnp.bfloat16),
    ]
    out = pl.pallas_call(
        functools.partial(build_kernel, layers, width),
        grid_spec=pltpu.PrefetchScalarGridSpec(
            num_scalar_prefetch=1,
            grid=(1,),
            in_specs=[pl.BlockSpec((6, layers, width), lambda i, t: (0, 0, t[0]))],
            out_specs=[pl.BlockSpec(memory_space=pltpu.VMEM)] * 3,
            scratch_shapes=[
                pltpu.VMEM((2 * layers + 1, 8, width), jnp.float32),
                pltpu.VMEM((2 * layers + 1, 6, GY, TILE), jnp.float32),
            ],
        ),
        out_shape=shapes,
        compiler_params=pltpu.CompilerParams(vmem_limit_bytes=6 << 20),
        cost_estimate=pl.CostEstimate(flops=20 << 20, bytes_accessed=24 << 20, transcendentals=0),
        name="build",
    )(place, moments)
    return [in_vmem(x) for x in out]


def image_kernel(layers, width, parts, index, blocks, *refs):
    refs = list(refs)
    pieces = [refs.pop(0) for _ in range(parts)]
    first_ref, rest_ref = pieces[0], pieces[-1]
    offset = 0 if parts == 2 else 3 * width + EDGE
    top_ref, plane_ref, edge_ref, corner_ref = (refs.pop(0) for _ in range(4))
    before = [(refs.pop(0), refs.pop(0)) for _ in range(index)]
    last = index == blocks - 1
    if last:
        block_refs = [refs.pop(0) for _ in range(index)]
        small_ref, place = refs.pop(0), refs.pop(0)
        keep_ref, send_ref, values_ref, image_ref = refs
    else:
        values_ref, image_ref, block_ref = refs
    f32, bf16 = jnp.float32, jnp.bfloat16
    depth = 3 * (layers + 1) * width
    rows = first_ref.shape[0]
    values_ref[:, : 3 * width] = first_ref[:, : 3 * width]
    values_ref[:, 3 * width : 3 * layers * width] = rest_ref[:, offset:]
    values_ref[:, 3 * layers * width : depth] = top_ref[:, : 3 * width]
    lane = lane_of((rows, EDGE))
    group = lane // GY
    halo = first_ref[:, 3 * width : 3 * width + EDGE].astype(f32)
    top = pltpu.roll(top_ref[:, 3 * width :].astype(f32), layers * GY, 1)
    halo = jnp.where(group % (layers + 1) == layers, top, halo)
    halo = jnp.where(group < 3 * (layers + 1), halo, 0.0).astype(bf16)
    values_ref[:, depth:] = halo

    def dot(a, b):
        return jnp.dot(a, b, preferred_element_type=f32)

    for z in range(layers + 1):
        for k in range(3):
            lo = (3 * z + k) * width
            hi = min(3 * (z + 2) * width, depth)
            value = values_ref[:, lo:hi]
            start = tile_start(k, 0, k) * width
            total = dot(halo, edge_ref[0, 3 * z + k]) + dot(halo, edge_ref[1, 3 * z + k])
            for term in range(2):
                total = total + dot(value, plane_ref[z, term, start : start + hi - lo, :])
            image_ref[:, lo : lo + width] = total.astype(bf16)
    image_ref[:, depth:] = (dot(halo, corner_ref[0]) + dot(halo, corner_ref[1])).astype(bf16)

    def product(a, b):
        return lax.dot_general(a[...], b[...], (((1,), (1,)), ((), ())), preferred_element_type=f32)

    found = [product(v, image_ref) + product(i, values_ref) for v, i in before]
    own = product(values_ref, image_ref)
    found.append(own + own.T)
    if not last:
        for j, value in enumerate(found):
            block_ref[j] = value
        return
    half = rows // 2
    for i in range(blocks):
        at = pl.ds(pl.multiple_of((i ^ place[1]) * half, half), half)
        for j in range(blocks):
            lo, hi = min(i, j), max(i, j)
            block = found[lo] if hi == index else block_refs[hi][lo]
            block = block.T if i > j else block
            for ref, low in ((keep_ref, 0), (send_ref, 1)):
                ref[at, j * rows : (j + 1) * rows] = jnp.where(place[0] == low, block[:half], block[half:])
    for j in range(blocks):
        for ref in (keep_ref, send_ref):
            ref[blocks * half :, j * rows : (j + 1) * rows] = small_ref[...]


def image_piece(index, piece, top, matrix, before, blocks, small, place, n_col):
    cols = top.shape[0]
    width = (top.shape[1] - EDGE) // 3
    layers = (sum(x.shape[1] for x in piece) - EDGE) // (3 * width)
    total = 3 * (layers + 1) * width + EDGE
    args = [*piece, top, *matrix, *(x for pair in before for x in pair)]
    shape = pltpu.VMEM((cols, total), top.dtype)
    scratch = []
    vmem = pl.BlockSpec(memory_space=pltpu.VMEM)
    in_specs = [vmem] * len(args)
    if index == n_col - 1:
        args += [*blocks, small, place]
        in_specs += [vmem] * (len(blocks) + 1) + [pl.BlockSpec(memory_space=pltpu.SMEM)]
        outs = [pltpu.VMEM((cols * n_col // 2 + small.shape[0], cols * n_col), jnp.float32)] * 2
        scratch = [shape] * 2
    else:
        outs = [shape, shape, pltpu.VMEM((index + 1, cols, cols), jnp.float32)]
    flops = 2 * 164 * cols * width * width + 4 * (index + 1) * cols * cols * total
    out = pl.pallas_call(
        functools.partial(image_kernel, layers, width, len(piece), index, n_col),
        in_specs=in_specs,
        out_specs=[vmem] * len(outs),
        out_shape=outs,
        scratch_shapes=scratch,
        compiler_params=pltpu.CompilerParams(vmem_limit_bytes=8 << 20),
        cost_estimate=pl.CostEstimate(flops=flops, bytes_accessed=24 << 20, transcendentals=0),
        name="image",
    )(*args)
    return out if index == n_col - 1 else [in_vmem(x) for x in out]


def small_sums(sensitivity, residual_force, zone_label, misfit, me, n_col, width):
    cols = sensitivity.shape[1]
    grad_part = lax.dot_general(
        residual_force,
        sensitivity,
        (((0, 1), (0, 2)), ((), ())),
        preferred_element_type=jnp.float32,
    )
    grad_full = lax.dynamic_update_slice_in_dim(jnp.zeros((width,), jnp.float32), grad_part, me * cols, 0)
    elements = zone_label.size
    share = elements // n_col
    offset = me * share
    zone_part = lax.dynamic_slice_in_dim(zone_label.reshape(elements), offset, share, 0)
    misfit_part = lax.dynamic_slice_in_dim(misfit.reshape(elements), offset, share, 0)
    onehot = (zone_part[:, None] == jnp.arange(width, dtype=jnp.int32)[None, :]).astype(jnp.float32)
    zone_part_sum = jnp.dot(misfit_part, onehot, precision=lax.Precision.HIGHEST)
    return jnp.concatenate([grad_full, zone_part_sum]).reshape(-1, cols)


def on_device(sensitivity, residual_force, moments, zone_label, misfit):
    cols = sensitivity.shape[1]
    layers = moments.shape[1]
    plane = GX * GY
    n_slab = lax.axis_size("slab")
    n_col = lax.axis_size("col")
    assert n_slab == 2 * n_col
    width = cols * n_col
    me = lax.axis_index("col").astype(jnp.int32)
    slab = lax.axis_index("slab").astype(jnp.int32)
    core, level_z = slab % 2, slab // 2

    source = pltpu.with_memory_space_constraint(sensitivity, pltpu.HBM)
    bottom = 3 * (plane // n_col) + EDGE
    pieces = [None] * n_col
    order = [*range(1, n_col), 0, 0]
    target = jnp.reshape(me ^ order[0], (1,))
    for k, follow in zip(order[:-1], order[1:]):
        *packed, target = pack(source, target, k ^ follow, layers, plane, n_col, k == n_col - 1)
        pieces[k] = [exchange(x, "col", k) for x in packed] if k else packed
    target, residual_force, misfit = lax.optimization_barrier((target, residual_force, misfit))
    small = small_sums(sensitivity, residual_force, zone_label, misfit, me, n_col, width)
    matrix = build(moments, target, plane // n_col)
    place = jnp.stack([core, me ^ level_z])
    before, blocks = [], []
    for k in range(n_col):
        low = crop(pieces[k][0], bottom, blocks[0]) if k else pieces[k][0][:, :bottom]
        top = shifted(low, "slab", -1)
        out = image_piece(k, pieces[k], top, matrix, before, blocks, small, place, n_col)
        if k < n_col - 1:
            before.append(out[:2])
            blocks.append(out[2])
    keep, send = out

    mine = keep + exchange(send, "slab", 1)
    parts = [mine[:, k * cols : (k + 1) * cols] for k in range(n_col)]
    mine = parts[0]
    for k in range(1, n_col):
        mine = mine + exchange(parts[k], "col", k)
    half, rows = cols // 2, width // 2
    parts = [jnp.concatenate([mine[k * half : (k + 1) * half], mine[rows:]]) for k in range(n_col)]
    mine = parts[0]
    for k in range(1, n_col):
        mine = mine + exchange(parts[k], "slab", 2 * k)
    hessian = mine[:half].T
    both = mine[half:].reshape(2, width)
    gradient = both[0]
    zone_misfit = both[1] * (width / (layers * plane * n_slab))
    return (hessian, gradient, zone_misfit)


def solution(mesh):
    in_specs = (
        P(None, "col", "slab"),
        P(None, "slab"),
        P(None, "slab", None),
        P("slab", None),
        P("slab", None),
    )
    out_specs = (P("col", "slab"), P(), P())
    return jax.shard_map(
        on_device, mesh=mesh, in_specs=in_specs, out_specs=out_specs, check_vma=False
    )
```

```python
import functools

import jax
import jax.numpy as jnp
from jax import lax
from jax.experimental import pallas as pl
from jax.experimental.pallas import tpu as pltpu
from jax.sharding import PartitionSpec as P

GX = 64
GY = 16
TILE = 128
EDGE = 256


def exchange(value, axis, by):
    count = lax.axis_size(axis)
    return lax.ppermute(value, axis, [(i, i ^ by) for i in range(count)])


def shifted(value, axis, by):
    count = lax.axis_size(axis)
    pairs = [(i, i + by) for i in range(count) if 0 <= i + by < count]
    return lax.ppermute(value, axis, pairs)


def lane_of(shape):
    return lax.broadcasted_iota(jnp.int32, shape, 1)


def pack_kernel(layers, plane, n_col, labels, cuts, me, sens_ref, *refs):
    outs, (planes, edges, sems, edge_sems) = refs[:-4], refs[-4:]
    next_ref, outs = outs[-1], list(outs[:-1])
    width = plane // n_col
    for i in range(3):
        next_ref[i] = me[i]
    top_block = layers * plane // TILE - 1
    rows = sens_ref.shape[1]
    pending = {}
    for index, label in enumerate(labels):
        target = me[0] ^ label
        for level in range(layers):
            source = pl.ds(pl.multiple_of((level * n_col + target) * width, width), width)
            block = jnp.minimum((level * plane + (target + 1) * width) // TILE, top_block)
            edge = pl.ds(pl.multiple_of(block * TILE, TILE), TILE)
            copies = (
                pltpu.make_async_copy(sens_ref.at[:, :, source], planes.at[index, level], sems.at[index, level]),
                pltpu.make_async_copy(sens_ref.at[:, :, edge], edges.at[index, level], edge_sems.at[index, level]),
            )
            for copy in copies:
                copy.start()
            pending[index, level] = copies
    lane = lane_of((rows, TILE))
    for index, (label, cut) in enumerate(zip(labels, cuts)):
        arrays = [outs.pop(0) for _ in range(2 if cut else 1)]

        def put(start, value):
            array = arrays[0]
            if start >= array.shape[1]:
                start, array = start - array.shape[1], arrays[1]
            array[:, start : start + value.shape[1]] = value

        inside = (me[0] ^ label) != n_col - 1
        halo = [jnp.zeros((rows, TILE), jnp.float32)] * (EDGE // TILE)
        for level in range(layers):
            for copy in pending[index, level]:
                copy.wait()
            for k in range(3):
                start = (3 * level + k) * width + (EDGE if level else 0)
                put(start, planes[index, level, k])
                tile, at = divmod(edge_at(k, level, layers), TILE)
                edge = edges[index, level, k].astype(jnp.float32)
                edge = pltpu.roll(edge, at, 1) if at else edge
                halo[tile] = jnp.where((lane >= at) & (lane < at + GY) & inside, edge, halo[tile])
        for tile, value in enumerate(halo):
            put(3 * width + tile * TILE, value.astype(sens_ref.dtype))


def edge_at(k, level, layers):
    return (k * (layers + 1) + level) * GY


def pack(sensitivity, me, labels, cuts, layers, plane, n_col):
    cols, dtype = sensitivity.shape[1], sensitivity.dtype
    width = plane // n_col
    outs, counts = [], []
    for cut in cuts:
        sizes = [3 * cut * width + EDGE, 3 * (layers - cut) * width] if cut else [3 * layers * width + EDGE]
        outs += [jax.ShapeDtypeStruct((cols, size), dtype) for size in sizes]
        counts.append(len(sizes))
    count = len(labels)
    *found, me = pl.pallas_call(
        functools.partial(pack_kernel, layers, plane, n_col, labels, cuts),
        in_specs=[pl.BlockSpec(memory_space=pltpu.SMEM), pl.BlockSpec(memory_space=pltpu.HBM)],
        out_specs=[pl.BlockSpec(memory_space=pltpu.VMEM)] * len(outs) + [pl.BlockSpec(memory_space=pltpu.SMEM)],
        out_shape=[*outs, jax.ShapeDtypeStruct((3,), jnp.int32)],
        scratch_shapes=[
            pltpu.VMEM((count, layers, 3, cols, width), dtype),
            pltpu.VMEM((count, layers, 3, cols, TILE), dtype),
            pltpu.SemaphoreType.DMA((count, layers)),
            pltpu.SemaphoreType.DMA((count, layers)),
        ],
        compiler_params=pltpu.CompilerParams(vmem_limit_bytes=8 << 20),
        cost_estimate=pl.CostEstimate(flops=0, bytes_accessed=6 << 20, transcendentals=0),
        name="pack",
    )(me, sensitivity)
    return [[found.pop(0) for _ in range(size)] for size in counts], me


def crop_kernel(piece_ref, _, out_ref):
    out_ref[...] = piece_ref[:, : out_ref.shape[1]]


def crop(piece, size, after):
    return pl.pallas_call(
        crop_kernel,
        in_specs=[pl.BlockSpec(memory_space=pltpu.VMEM), pl.BlockSpec(memory_space=pl.ANY)],
        out_specs=pl.BlockSpec(memory_space=pltpu.VMEM),
        out_shape=jax.ShapeDtypeStruct((piece.shape[0], size), piece.dtype),
        compiler_params=pltpu.CompilerParams(vmem_limit_bytes=8 << 20),
        cost_estimate=pl.CostEstimate(flops=0, bytes_accessed=0, transcendentals=0),
        name="crop",
    )(piece, after)


def component(a, b):
    a, b = min(a, b), max(a, b)
    return a if a == b else a + b + 2


def tile_start(z, k, side, other, layers):
    base = 15 * z + ((0, 6, 11)[k] if z < layers else (0, 3, 5)[k])
    return base + (other - k if side == 0 else 3 - k + other)


def build_kernel(layers, width, _, moments_ref, after_ref, plane_ref, edge_ref, corner_ref, field_ref, ahead_ref):
    f32, bf16 = jnp.float32, jnp.bfloat16
    shape = (GY, width)
    lane = lane_of(shape)
    row = lax.broadcasted_iota(jnp.int32, shape, 0)
    pos_x, pos_y = lane // GY, lane % GY
    same, up, down = row == pos_y, row == pos_y + 1, row == pos_y - 1
    zero = jnp.zeros(shape, f32)
    field_lane = lane_of((8, width))
    columns = width // GY
    near = [pos_x % 3 == r for r in range(3)]
    follow = [(pos_x + 1) % 3 == r for r in range(3)]
    band = [jnp.where((pos_x >= x - 1) & (pos_x <= x + 1), 1.0, 0.0).astype(bf16) for x in range(columns)]
    tile_lane = lane_of((GY, TILE))

    def spread(middle, ahead, behind):
        def whole(value):
            return jnp.broadcast_to(value, shape)

        return jnp.where(same, whole(middle), jnp.where(up, whole(ahead), jnp.where(down, whole(behind), zero)))

    def two_terms(value):
        hi = value.astype(bf16)
        return hi, (value - hi.astype(f32)).astype(bf16)

    edge_ref[...] = jnp.zeros_like(edge_ref)
    field_ref[...] = jnp.zeros_like(field_ref)
    for z in range(layers + 1):
        whole = None
        for level in (z, z - 1):
            if 0 <= level < layers:
                part = moments_ref[:, level, :] * (2.0 / 216.0)
                whole = part if whole is None else whole + part
        field_ref[2 * z, :6] = whole
        if z < layers:
            field_ref[2 * z + 1, :6] = moments_ref[:, z, :] * (1.0 / 216.0)

    for pair in range(2 * layers + 1):
        z, side = divmod(pair, 2)
        element = field_ref[pair]
        before = jnp.where(field_lane >= GY, pltpu.roll(element, GY, 1), 0.0)
        parts = []
        for value in (2.0 * (element + before), element, before):
            lower = jnp.where(field_lane % GY != 0, pltpu.roll(value, 1, 1), 0.0)
            parts.append((2.0 * (value + lower), value, lower))
        for c in range(6):
            here, ahead, behind = [spread(*(v[c : c + 1] for v in part)) for part in parts]
            ahead_ref[pair, c] = ahead[:, width - TILE :]
            scale = 0.5 if side == 0 and c < 3 else None
            spots = []
            for k in range(3):
                for other in range(3):
                    if component(k, other) == c and (side == 1 or other >= k):
                        spots.append(tile_start(z, k, side, other, layers))
            for r in range(3):
                value = jnp.where(near[r], here, jnp.where(follow[r], ahead, behind))
                if scale is not None:
                    value = value * scale
                for term, piece in enumerate(two_terms(value)):
                    for x in range(r, columns, 3):
                        block = piece * band[x]
                        for spot in spots:
                            start = spot * width + x * GY
                            plane_ref[term, start : start + GY, :] = block

    edge_lane = tile_lane // GY == TILE // GY - 1
    for z in range(layers + 1):
        for other_z in range(max(z - 1, 0), min(z + 1, layers) + 1):
            pair = 2 * z if other_z == z else 2 * min(z, other_z) + 1
            for c in range(6):
                value = jnp.where(edge_lane, ahead_ref[pair, c], 0.0)
                for term, piece in enumerate(two_terms(value)):
                    for k in range(3):
                        for other in range(3):
                            if component(k, other) == c:
                                start = edge_at(other, other_z, layers)
                                edge_ref[term, 3 * z + k, start : start + GY, :] = piece

    corner_ref[...] = jnp.zeros_like(corner_ref)
    for other_z in range(layers + 1):
        for other in range(3):
            tiles = [jnp.zeros((GY, TILE), f32)] * (EDGE // TILE)
            for z in range(max(other_z - 1, 0), min(other_z + 1, layers) + 1):
                pair = 2 * z if other_z == z else 2 * min(z, other_z) + 1
                for k in range(3):
                    tile, at = divmod(edge_at(k, z, layers), TILE)
                    value = ahead_ref[pair, component(k, other)]
                    turn = (at + GY) % TILE
                    value = pltpu.roll(value, turn, 1) if turn else value
                    tiles[tile] = jnp.where(tile_lane // GY == at // GY, value, tiles[tile])
            start = edge_at(other, other_z, layers)
            for tile, value in enumerate(tiles):
                for term, piece in enumerate(two_terms(value)):
                    corner_ref[term, start : start + GY, tile * TILE : (tile + 1) * TILE] = piece


def in_vmem(x):
    return pltpu.with_memory_space_constraint(x, pltpu.VMEM)


def build(moments, place, width, after):
    layers = moments.shape[1]
    shapes = [
        pltpu.VMEM((2, (15 * layers + 6) * width, width), jnp.bfloat16),
        pltpu.VMEM((2, 3 * (layers + 1), EDGE, TILE), jnp.bfloat16),
        pltpu.VMEM((2, EDGE, EDGE), jnp.bfloat16),
    ]
    out = pl.pallas_call(
        functools.partial(build_kernel, layers, width),
        grid_spec=pltpu.PrefetchScalarGridSpec(
            num_scalar_prefetch=1,
            grid=(1,),
            in_specs=[
                pl.BlockSpec((6, layers, width), lambda i, t: (0, 0, t[0])),
                pl.BlockSpec(memory_space=pl.ANY),
            ],
            out_specs=[pl.BlockSpec(memory_space=pltpu.VMEM)] * 3,
            scratch_shapes=[
                pltpu.VMEM((2 * layers + 1, 8, width), jnp.float32),
                pltpu.VMEM((2 * layers + 1, 6, GY, TILE), jnp.float32),
            ],
        ),
        out_shape=shapes,
        compiler_params=pltpu.CompilerParams(vmem_limit_bytes=8 << 20),
        cost_estimate=pl.CostEstimate(flops=0, bytes_accessed=0, transcendentals=0),
        name="build",
    )(place, moments, after)
    return [in_vmem(x) for x in out]


def image_kernel(layers, width, parts, label, seen, *refs):
    refs = list(refs)
    pieces = [refs.pop(0) for _ in range(parts)]
    first_ref = pieces[0]
    top_ref, plane_ref, edge_ref, corner_ref = (refs.pop(0) for _ in range(4))
    before = [(refs.pop(0), refs.pop(0)) for _ in seen]
    blocks = len(seen) + 1
    block_refs = None
    if len(refs) > 3:
        block_refs = [refs.pop(0) for _ in seen]
        small_ref, place = refs.pop(0), refs.pop(0)
        keep_ref, send_ref, values_ref, image_ref = refs
    else:
        values_ref, image_ref, block_ref = refs
    f32, bf16 = jnp.float32, jnp.bfloat16
    depth = 3 * (layers + 1) * width
    rows = first_ref.shape[0]

    values_ref[:, : 3 * width] = first_ref[:, : 3 * width]
    begin = 3 * width
    for array, skip in zip(pieces, (3 * width + EDGE, 0)):
        if skip < array.shape[1]:
            end = begin + array.shape[1] - skip
            values_ref[:, begin:end] = array[:, skip:]
            begin = end
    values_ref[:, 3 * layers * width : depth] = top_ref[:, : 3 * width]
    lane = lane_of((rows, EDGE))
    group = lane // GY
    halo = first_ref[:, 3 * width : 3 * width + EDGE].astype(f32)
    top = pltpu.roll(top_ref[:, 3 * width :].astype(f32), layers * GY, 1)
    halo = jnp.where(group % (layers + 1) == layers, top, halo)
    halo = jnp.where(group < 3 * (layers + 1), halo, 0.0).astype(bf16)
    values_ref[:, depth:] = halo

    def dot(a, b):
        return jnp.dot(a, b, preferred_element_type=f32)

    for z in range(layers + 1):
        for k in range(3):
            lo = (3 * z + k) * width
            hi = min(3 * (z + 2) * width, depth)
            value = values_ref[:, lo:hi]
            start = tile_start(z, k, 0, k, layers) * width
            matrix = plane_ref.at[:, start : start + hi - lo, :]
            total = dot(value, matrix[0]) + dot(value, matrix[1])
            edge = dot(halo, edge_ref[0, 3 * z + k]) + dot(halo, edge_ref[1, 3 * z + k])
            inner = width - TILE
            if inner:
                image_ref[:, lo : lo + inner] = total[:, :inner].astype(bf16)
            image_ref[:, lo + inner : lo + width] = (total[:, inner:] + edge).astype(bf16)
    image_ref[:, depth:] = (dot(halo, corner_ref[0]) + dot(halo, corner_ref[1])).astype(bf16)

    def product(a, b):
        return lax.dot_general(a[...], b[...], (((1,), (1,)), ((), ())), preferred_element_type=f32)

    found = [product(v, image_ref) + product(i, values_ref) for v, i in before]
    own = product(values_ref, image_ref)
    found.append(own + own.T)
    if block_refs is None:
        for j, value in enumerate(found):
            block_ref[j] = value
        return
    half = rows // 2
    order = [*seen, label]
    for i in range(blocks):
        at = pl.ds(pl.multiple_of((i ^ place[2]) * half, half), half)
        for j in range(blocks):
            lo, hi = sorted((order.index(i), order.index(j)))
            block = found[lo] if hi == blocks - 1 else block_refs[hi][lo]
            block = block.T if order.index(i) > order.index(j) else block
            for ref, low in ((keep_ref, 0), (send_ref, 1)):
                ref[at, j * rows : (j + 1) * rows] = jnp.where(place[1] == low, block[:half], block[half:])
    for j in range(blocks):
        for ref in (keep_ref, send_ref):
            ref[blocks * half :, j * rows : (j + 1) * rows] = small_ref[...]


def image_piece(label, seen, piece, top, matrix, before, blocks, small, place, n_col):
    cols = top.shape[0]
    width = (top.shape[1] - EDGE) // 3
    layers = (sum(x.shape[1] for x in piece) - EDGE) // (3 * width)
    total = 3 * (layers + 1) * width + EDGE
    vmem = pl.BlockSpec(memory_space=pltpu.VMEM)
    args = [*piece, top, *matrix, *(x for pair in before for x in pair)]
    in_specs = [vmem] * (len(piece) + 4 + 2 * len(before))
    shape = pltpu.VMEM((cols, total), top.dtype)
    scratch = []
    last = len(seen) == n_col - 1
    if last:
        args += [*blocks, small, place]
        in_specs += [vmem] * (len(blocks) + 1) + [pl.BlockSpec(memory_space=pltpu.SMEM)]
        outs = [pltpu.VMEM((cols * n_col // 2 + small.shape[0], cols * n_col), jnp.float32)] * 2
        scratch = [shape] * 2
    else:
        outs = [shape, shape, pltpu.VMEM((len(seen) + 1, cols, cols), jnp.float32)]
    out = pl.pallas_call(
        functools.partial(image_kernel, layers, width, len(piece), label, seen),
        in_specs=in_specs,
        out_specs=[vmem] * len(outs),
        out_shape=outs,
        scratch_shapes=scratch,
        compiler_params=pltpu.CompilerParams(vmem_limit_bytes=8 << 20),
        cost_estimate=pl.CostEstimate(flops=0, bytes_accessed=16 << 20, transcendentals=0),
        name="image",
    )(*args)
    return out if last else [in_vmem(x) for x in out]


def sums_kernel(blocks, me, sens_ref, force_ref, label_ref, misfit_ref, out_ref):
    step = pl.program_id(0)
    f32, bf16 = jnp.float32, jnp.bfloat16
    cols = sens_ref.shape[1]
    contract = (((1,), (1,)), ((), ()))

    @pl.when(step == 0)
    def _():
        layers, width = label_ref.shape
        row = lax.broadcasted_iota(jnp.int32, (8, width), 0)
        zone = lax.broadcasted_iota(jnp.int32, (cols, width), 0)
        out_ref[:blocks] = jnp.zeros((blocks, cols), f32)
        for b in range(blocks):
            total = jnp.zeros((8, cols), f32)
            for level in range(layers):
                value = jnp.broadcast_to(misfit_ref[level : level + 1], (8, width))
                high = value.astype(bf16).astype(f32)
                middle = (value - high).astype(bf16).astype(f32)
                low = value - high - middle
                terms = jnp.where(row == 0, high, jnp.where(row == 1, middle, jnp.where(row == 2, low, 0.0)))
                label = jnp.broadcast_to(label_ref[level : level + 1], (cols, width))
                chosen = jnp.where(label == zone + b * cols, 1.0, 0.0).astype(bf16)
                total += lax.dot_general(terms.astype(bf16), chosen, contract, preferred_element_type=f32)
            out_ref[blocks + b : blocks + b + 1] = jnp.sum(total, axis=0, keepdims=True)

    grad = lax.dot_general(force_ref[...], sens_ref[0], contract, preferred_element_type=f32)
    part = lax.broadcasted_iota(jnp.int32, grad.shape, 0)
    grad = jnp.sum(jnp.where(part == step, grad, 0.0), axis=0, keepdims=True)
    block = lax.broadcasted_iota(jnp.int32, (blocks, cols), 0)
    out_ref[:blocks] += jnp.where(block == me[0], jnp.broadcast_to(grad, (blocks, cols)), 0.0)


def small_sums(sensitivity, residual_force, zone_label, misfit, me, n_col):
    _, cols, nodes = sensitivity.shape
    layers, plane = zone_label.shape
    width = plane // n_col
    return pl.pallas_call(
        functools.partial(sums_kernel, n_col),
        grid_spec=pltpu.PrefetchScalarGridSpec(
            num_scalar_prefetch=1,
            grid=(3,),
            in_specs=[
                pl.BlockSpec((1, cols, nodes), lambda i, t: (i, 0, 0)),
                pl.BlockSpec((3, nodes), lambda i, t: (0, 0)),
                pl.BlockSpec((layers, width), lambda i, t: (0, t[0])),
                pl.BlockSpec((layers, width), lambda i, t: (0, t[0])),
            ],
            out_specs=pl.BlockSpec((2 * n_col, cols), lambda i, t: (0, 0)),
        ),
        out_shape=jax.ShapeDtypeStruct((2 * n_col, cols), jnp.float32),
        compiler_params=pltpu.CompilerParams(vmem_limit_bytes=8 << 20),
        cost_estimate=pl.CostEstimate(flops=0, bytes_accessed=12 << 20, transcendentals=0),
        name="sums",
    )(me, sensitivity, residual_force, zone_label, misfit)


def on_device(sensitivity, residual_force, moments, zone_label, misfit):
    cols = sensitivity.shape[1]
    layers = moments.shape[1]
    plane = GX * GY
    n_slab = lax.axis_size("slab")
    n_col = lax.axis_size("col")
    assert n_slab == 2 * n_col
    width = cols * n_col
    me = lax.axis_index("col").astype(jnp.int32)
    slab = lax.axis_index("slab").astype(jnp.int32)
    core, level_z = slab % 2, slab // 2

    source = pltpu.with_memory_space_constraint(sensitivity, pltpu.HBM)
    bottom = 3 * (plane // n_col) + EDGE
    last = n_col - 1
    order = sorted(range(1, n_col), key=lambda k: (k.bit_count(), -k))
    single = [k for k in order if k.bit_count() == 1]
    double = [k for k in order if k.bit_count() > 1] + [0]
    place = jnp.stack([me, core, me ^ level_z])
    pieces, before, blocks, seen = {}, [], [], []
    for labels in (single, double):
        packed, place = pack(source, place, labels, [1 if k == 0 else layers // 2 if k == last else 0 for k in labels], layers, plane, n_col)
        for k, piece in zip(labels, packed):
            pieces[k] = [exchange(x, "col", k) for x in piece] if k else piece
    small = small_sums(source, residual_force, zone_label, misfit, place, n_col)
    matrix = build(moments, place, plane // n_col, small)
    for k in (0, *order):
        low = crop(pieces[k][0], bottom, blocks[1 if k == last else 0]) if k else pieces[k][0]
        top = shifted(low, "slab", -1)
        out = image_piece(k, tuple(seen), pieces[k], top, matrix, before, blocks, small, place, n_col)
        seen.append(k)
        if len(seen) < n_col:
            before.append(out[:2])
            blocks.append(out[2])
    keep, send = out

    mine = keep + exchange(send, "slab", 1)
    parts = [mine[:, k * cols : (k + 1) * cols] for k in range(n_col)]
    mine = parts[0]
    for k in range(1, n_col):
        mine = mine + exchange(parts[k], "col", k)
    half = cols // 2
    count = n_col
    while count > 1:
        count //= 2
        near, far, extra = mine[: count * half], mine[count * half : 2 * count * half], mine[2 * count * half :]
        mine = jnp.concatenate([near, extra]) + exchange(jnp.concatenate([far, extra]), "slab", 2 * count)
    hessian = mine[:half].T
    both = mine[half:].reshape(2, width)
    gradient = both[0]
    zone_misfit = both[1] * (width / (layers * plane * n_slab))
    return (hessian, gradient, zone_misfit)


def solution(mesh):
    in_specs = (
        P(None, "col", "slab"),
        P(None, "slab"),
        P(None, "slab", None),
        P("slab", None),
        P("slab", None),
    )
    out_specs = (P("col", "slab"), P(), P())
    return jax.shard_map(
        on_device, mesh=mesh, in_specs=in_specs, out_specs=out_specs, check_vma=False
    )
```

```python
import functools

import jax
import jax.numpy as jnp
from jax import lax
from jax.experimental import pallas as pl
from jax.experimental.pallas import tpu as pltpu
from jax.sharding import PartitionSpec as P

GX = 64
GY = 16
TILE = 128
EDGE = 256


def exchange(value, axis, by):
    count = lax.axis_size(axis)
    return lax.ppermute(value, axis, [(i, i ^ by) for i in range(count)])


def shifted(value, axis, by):
    count = lax.axis_size(axis)
    pairs = [(i, i + by) for i in range(count) if 0 <= i + by < count]
    return lax.ppermute(value, axis, pairs)


def lane_of(shape):
    return lax.broadcasted_iota(jnp.int32, shape, 1)


def pack_kernel(layers, plane, n_col, specs, after, sens_ref, *refs):
    outs, (planes, sems) = refs[:-2], refs[-2:]
    col, slab = lax.axis_index("col"), lax.axis_index("slab")
    outs = list(outs)
    next_ref = outs.pop()
    outs = outs[after:]
    width = plane // n_col
    for i, value in enumerate((col, slab % 2, col ^ (slab // 2))):
        next_ref[i] = value
    inner, both = slice(0, width), slice(0, width + TILE)
    slots, waits = {}, {}
    for label in dict.fromkeys(spec[0] for spec in specs):
        spans = [levels for name, levels, _ in specs if name == label]
        edges = any(levels[0] == 0 for levels in spans)
        for level in range(layers):
            held = any(level in levels for levels in spans)
            if not (held or edges):
                continue
            target = col ^ label
            slot = slots[label, level] = len(slots)
            start = pl.multiple_of((level * n_col + target) * width, width)

            def copy(part, start=start, slot=slot):
                source = sens_ref.at[:, :, pl.ds(start + part.start, part.stop - part.start)]
                return pltpu.make_async_copy(source, planes.at[slot, :, :, part], sems.at[slot])

            inside = target != n_col - 1
            if not edges:
                cases = [(None, inner)]
            elif held:
                cases = [(inside, both), (jnp.logical_not(inside), inner)]
            else:
                cases = [(inside, slice(width, width + TILE))]
            for case, part in cases:
                if case is None:
                    copy(part).start()
                else:
                    pl.when(case)(copy(part).start)
            waits[label, level] = [(case, copy(part)) for case, part in cases]
    dtype = sens_ref.dtype
    for array, (label, levels, rows) in zip(outs, specs):
        lane = lane_of((rows[1] - rows[0], TILE))
        halo = [jnp.zeros(lane.shape, jnp.float32)] * (EDGE // TILE)
        start = 0
        for level in range(layers):
            if level not in levels and levels[0]:
                continue
            for case, copy in waits.pop((label, level), ()):
                if case is None:
                    copy.wait()
                else:
                    pl.when(case)(copy.wait)
            for k in range(3):
                piece = planes.at[slots[label, level], k, rows[0] : rows[1]]
                if level in levels:
                    array[:, start : start + width] = piece[:, inner]
                    start += width
                if levels[0] == 0:
                    tile, at = divmod(edge_at(k, level, layers), TILE)
                    edge = piece[:, width:].astype(jnp.float32)
                    edge = pltpu.roll(edge, at, 1) if at else edge
                    keep = (lane >= at) & (lane < at + GY) & ((col ^ label) != n_col - 1)
                    halo[tile] = jnp.where(keep, edge, halo[tile])
            if level == 0:
                start += EDGE
        if levels[0] == 0:
            for tile, value in enumerate(halo):
                begin = 3 * width + tile * TILE
                array[:, begin : begin + TILE] = value.astype(dtype)


def edge_at(k, level, layers):
    return (k * (layers + 1) + level) * GY


def pack(sensitivity, after, specs, layers, plane, n_col):
    cols, dtype = sensitivity.shape[1], sensitivity.dtype
    width = plane // n_col
    outs, slots = [], set()
    for label, levels, rows in specs:
        size = 3 * len(levels) * width + (0 if levels[0] else EDGE)
        outs.append(jax.ShapeDtypeStruct((rows[1] - rows[0], size), dtype))
        slots |= {(label, level) for level in (levels if levels[0] else range(layers))}
    *found, place = pl.pallas_call(
        functools.partial(pack_kernel, layers, plane, n_col, specs, len(after)),
        in_specs=[pl.BlockSpec(memory_space=pltpu.HBM)] + [pl.BlockSpec(memory_space=pltpu.SMEM)] * len(after),
        out_specs=[pl.BlockSpec(memory_space=pltpu.VMEM)] * len(outs) + [pl.BlockSpec(memory_space=pltpu.SMEM)],
        out_shape=[*outs, jax.ShapeDtypeStruct((3,), jnp.int32)],
        scratch_shapes=[
            pltpu.VMEM((len(slots), 3, cols, width + TILE), dtype),
            pltpu.SemaphoreType.DMA((len(slots),)),
        ],
        compiler_params=pltpu.CompilerParams(vmem_limit_bytes=8 << 20),
        cost_estimate=pl.CostEstimate(flops=0, bytes_accessed=4 << 20, transcendentals=0),
        name="pack",
    )(sensitivity, *after)
    return found, place


def crop_kernel(piece_ref, _, out_ref):
    out_ref[...] = piece_ref[:, : out_ref.shape[1]]


def crop(piece, size, after):
    return pl.pallas_call(
        crop_kernel,
        in_specs=[pl.BlockSpec(memory_space=pltpu.VMEM), pl.BlockSpec(memory_space=pl.ANY)],
        out_specs=pl.BlockSpec(memory_space=pltpu.VMEM),
        out_shape=jax.ShapeDtypeStruct((piece.shape[0], size), piece.dtype),
        compiler_params=pltpu.CompilerParams(vmem_limit_bytes=8 << 20),
        cost_estimate=pl.CostEstimate(flops=0, bytes_accessed=0, transcendentals=0),
        name="crop",
    )(piece, after)


def component(a, b):
    a, b = min(a, b), max(a, b)
    return a if a == b else a + b + 2


def tile_start(z, k, side, other, layers):
    base = 15 * z + ((0, 6, 11)[k] if z < layers else (0, 3, 5)[k])
    return base + (other - k if side == 0 else 3 - k + other)


def zone_sums(label_ref, misfit_ref, zone_ref):
    f32, bf16 = jnp.float32, jnp.bfloat16
    layers, width = label_ref.shape
    blocks, cols = zone_ref.shape
    row = lax.broadcasted_iota(jnp.int32, (8, width), 0)
    zone = lax.broadcasted_iota(jnp.int32, (cols, width), 0)
    for b in range(blocks):
        total = jnp.zeros((8, cols), f32)
        for level in range(layers):
            value = jnp.broadcast_to(misfit_ref[level : level + 1], (8, width))
            high = value.astype(bf16).astype(f32)
            middle = (value - high).astype(bf16).astype(f32)
            low = value - high - middle
            terms = jnp.where(row == 0, high, jnp.where(row == 1, middle, jnp.where(row == 2, low, 0.0)))
            label = jnp.broadcast_to(label_ref[level : level + 1], (cols, width))
            chosen = jnp.where(label == zone + b * cols, 1.0, 0.0).astype(bf16)
            total += lax.dot_general(
                terms.astype(bf16), chosen, (((1,), (1,)), ((), ())), preferred_element_type=f32
            )
        zone_ref[b : b + 1] = jnp.sum(total, axis=0, keepdims=True)


def build_kernel(layers, width, place, moments_ref, label_ref, misfit_ref, *refs):
    force_refs, refs = refs[:layers], refs[layers:]
    plane_ref, edge_ref, corner_ref, force_ref, zone_ref, field_ref, ahead_ref = refs
    f32, bf16 = jnp.float32, jnp.bfloat16
    force_ref[...] = jnp.zeros_like(force_ref)
    for z in range(layers):
        for k in range(3):
            value = force_refs[z][k : k + 1].astype(f32)
            start = (3 * z + k) * width
            force_ref[:, start : start + width] = jnp.broadcast_to(value, (16, width)).astype(bf16)
    zone_sums(label_ref, misfit_ref, zone_ref)
    shape = (GY, width)
    lane = lane_of(shape)
    row = lax.broadcasted_iota(jnp.int32, shape, 0)
    pos_x, pos_y = lane // GY, lane % GY
    same, up, down = row == pos_y, row == pos_y + 1, row == pos_y - 1
    zero = jnp.zeros(shape, f32)
    field_lane = lane_of((8, width))
    columns = width // GY
    near = [pos_x % 3 == r for r in range(3)]
    follow = [(pos_x + 1) % 3 == r for r in range(3)]
    band = [jnp.where((pos_x >= x - 1) & (pos_x <= x + 1), 1.0, 0.0).astype(bf16) for x in range(columns)]
    tile_lane = lane_of((GY, TILE))

    def spread(middle, ahead, behind):
        def whole(value):
            return jnp.broadcast_to(value, shape)

        return jnp.where(same, whole(middle), jnp.where(up, whole(ahead), jnp.where(down, whole(behind), zero)))

    def two_terms(value):
        hi = value.astype(bf16)
        return hi, (value - hi.astype(f32)).astype(bf16)

    edge_ref[...] = jnp.zeros_like(edge_ref)
    field_ref[...] = jnp.zeros_like(field_ref)
    for z in range(layers + 1):
        whole = None
        for level in (z, z - 1):
            if 0 <= level < layers:
                part = moments_ref[:, level, :] * (2.0 / 216.0)
                whole = part if whole is None else whole + part
        field_ref[2 * z, :6] = whole
        if z < layers:
            field_ref[2 * z + 1, :6] = moments_ref[:, z, :] * (1.0 / 216.0)

    for pair in range(2 * layers + 1):
        z, side = divmod(pair, 2)
        element = field_ref[pair]
        before = jnp.where(field_lane >= GY, pltpu.roll(element, GY, 1), 0.0)
        parts = []
        for value in (2.0 * (element + before), element, before):
            lower = jnp.where(field_lane % GY != 0, pltpu.roll(value, 1, 1), 0.0)
            parts.append((2.0 * (value + lower), value, lower))
        for c in range(6):
            here, ahead, behind = [spread(*(v[c : c + 1] for v in part)) for part in parts]
            ahead_ref[pair, c] = ahead[:, width - TILE :]
            scale = 0.5 if side == 0 and c < 3 else None
            spots = []
            for k in range(3):
                for other in range(3):
                    if component(k, other) == c and (side == 1 or other >= k):
                        spots.append(tile_start(z, k, side, other, layers))
            for r in range(3):
                value = jnp.where(near[r], here, jnp.where(follow[r], ahead, behind))
                if scale is not None:
                    value = value * scale
                for term, piece in enumerate(two_terms(value)):
                    for x in range(r, columns, 3):
                        block = piece * band[x]
                        for spot in spots:
                            start = spot * width + x * GY
                            plane_ref[term, start : start + GY, :] = block

    edge_lane = tile_lane // GY == TILE // GY - 1
    for z in range(layers + 1):
        for other_z in range(max(z - 1, 0), min(z + 1, layers) + 1):
            pair = 2 * z if other_z == z else 2 * min(z, other_z) + 1
            for c in range(6):
                value = jnp.where(edge_lane, ahead_ref[pair, c], 0.0)
                for term, piece in enumerate(two_terms(value)):
                    for k in range(3):
                        for other in range(3):
                            if component(k, other) == c:
                                start = edge_at(other, other_z, layers)
                                n, at = divmod(3 * z + k, 2)
                                edge_ref[term, n, start : start + GY, at * TILE : (at + 1) * TILE] = piece

    corner_ref[...] = jnp.zeros_like(corner_ref)
    for other_z in range(layers + 1):
        for other in range(3):
            tiles = [jnp.zeros((GY, TILE), f32)] * (EDGE // TILE)
            for z in range(max(other_z - 1, 0), min(other_z + 1, layers) + 1):
                pair = 2 * z if other_z == z else 2 * min(z, other_z) + 1
                for k in range(3):
                    tile, at = divmod(edge_at(k, z, layers), TILE)
                    value = ahead_ref[pair, component(k, other)]
                    turn = (at + GY) % TILE
                    value = pltpu.roll(value, turn, 1) if turn else value
                    tiles[tile] = jnp.where(tile_lane // GY == at // GY, value, tiles[tile])
            start = edge_at(other, other_z, layers)
            for tile, value in enumerate(tiles):
                for term, piece in enumerate(two_terms(value)):
                    corner_ref[term, start : start + GY, tile * TILE : (tile + 1) * TILE] = piece


def in_vmem(x):
    return pltpu.with_memory_space_constraint(x, pltpu.VMEM)


def build(moments, zone_label, misfit, residual_force, place, n_col, cols):
    layers, plane = zone_label.shape
    width = plane // n_col
    shapes = [
        ((2, (15 * layers + 6) * width, width), jnp.bfloat16),
        ((2, (3 * layers + 4) // 2, EDGE, 2 * TILE), jnp.bfloat16),
        ((2, EDGE, EDGE), jnp.bfloat16),
        ((16, 3 * (layers + 1) * width + EDGE), jnp.bfloat16),
        ((n_col, cols), jnp.float32),
    ]

    def force_spec(level):
        return pl.BlockSpec((3, width), lambda i, t: (0, level * n_col + t[0]))

    out = pl.pallas_call(
        functools.partial(build_kernel, layers, width),
        grid_spec=pltpu.PrefetchScalarGridSpec(
            num_scalar_prefetch=1,
            grid=(1,),
            in_specs=[
                pl.BlockSpec((6, layers, width), lambda i, t: (0, 0, t[0])),
                pl.BlockSpec((layers, width), lambda i, t: (0, t[0])),
                pl.BlockSpec((layers, width), lambda i, t: (0, t[0])),
            ]
            + [force_spec(level) for level in range(layers)],
            out_specs=[pl.BlockSpec(memory_space=pltpu.VMEM)] * len(shapes),
            scratch_shapes=[
                pltpu.VMEM((2 * layers + 1, 8, width), jnp.float32),
                pltpu.VMEM((2 * layers + 1, 6, GY, TILE), jnp.float32),
            ],
        ),
        out_shape=[pltpu.VMEM(*shape) for shape in shapes],
        compiler_params=pltpu.CompilerParams(vmem_limit_bytes=8 << 20),
        cost_estimate=pl.CostEstimate(flops=0, bytes_accessed=12 << 20, transcendentals=0),
        name="build",
    )(place, moments, zone_label, misfit, *([residual_force] * layers))
    return [in_vmem(x) for x in out]


def image_layers(layers, width, values_ref, image_ref, matrix):
    plane_ref, edge_ref, corner_ref = matrix
    f32, bf16 = jnp.float32, jnp.bfloat16
    depth = 3 * (layers + 1) * width
    halo = values_ref[:, depth:]

    def dot(a, b):
        return jnp.dot(a, b, preferred_element_type=f32)

    edges = []
    for n in range(edge_ref.shape[1]):
        both = dot(halo, edge_ref[0, n]) + dot(halo, edge_ref[1, n])
        edges += [both[:, :TILE], both[:, TILE:]]
    for z in range(layers + 1):
        for k in range(3):
            lo = (3 * z + k) * width
            hi = min(3 * (z + 2) * width, depth)
            start = tile_start(z, k, 0, k, layers) * width
            value, held = values_ref[:, lo:hi], plane_ref.at[:, start : start + hi - lo, :]
            total = dot(value, held[0]) + dot(value, held[1])
            inner = width - TILE
            if inner:
                image_ref[:, lo : lo + inner] = total[:, :inner].astype(bf16)
            image_ref[:, lo + inner : lo + width] = (total[:, inner:] + edges[3 * z + k]).astype(bf16)
    image_ref[:, depth:] = (dot(halo, corner_ref[0]) + dot(halo, corner_ref[1])).astype(bf16)


def copy_in(pieces, start, values_ref, width):
    for array in pieces:
        if start == 0:
            values_ref[:, : 3 * width] = array[:, : 3 * width]
            start, skip = 3 * width, 3 * width + EDGE
        else:
            skip = 0
        if skip < array.shape[1]:
            end = start + array.shape[1] - skip
            values_ref[:, start:end] = array[:, skip:]
            start = end


def halo_of(first_ref, top_ref, layers, width):
    group = lane_of((first_ref.shape[0], EDGE)) // GY
    halo = first_ref[:, 3 * width : 3 * width + EDGE].astype(jnp.float32)
    top = pltpu.roll(top_ref[:, 3 * width :].astype(jnp.float32), layers * GY, 1)
    halo = jnp.where(group % (layers + 1) == layers, top, halo)
    return jnp.where(group < 3 * (layers + 1), halo, 0.0).astype(jnp.bfloat16)


def product(a, b):
    return lax.dot_general(a, b, (((1,), (1,)), ((), ())), preferred_element_type=jnp.float32)


def products(held, values_ref, image_ref, slot):
    rows = values_ref.shape[0] // 2
    value, image = (ref[slot * rows : (slot + 1) * rows] for ref in (values_ref, image_ref))
    found = []
    for v, i in held:
        both = product(image, v[...]) + product(value, i[...])
        found += [both[:, :rows], both[:, rows:]]
    if slot:
        both = product(image, values_ref[...])
        found.append(both[:, :rows] + product(value, image_ref[:rows]))
        own = both[:, rows:]
    else:
        own = product(image, value)
    return [*found, own + own.T]


def fill(layers, width, pieces, top_ref, values_ref):
    depth = 3 * (layers + 1) * width
    copy_in(pieces, 0, values_ref, width)
    values_ref[:, 3 * layers * width : depth] = top_ref[:, : 3 * width]
    values_ref[:, depth:] = halo_of(pieces[0], top_ref, layers, width)


def image_kernel(layers, width, arrays, order, last, *refs):
    refs, (pair, slot) = list(refs), divmod(len(order) - 1, 2)
    place = refs.pop(0) if last else None
    pieces = [refs.pop(0) for _ in range(arrays)]
    top_ref, *matrix, force_ref = (refs.pop(0) for _ in range(5))
    held = [(refs.pop(0), refs.pop(0)) for _ in range(pair)]
    block_refs = [refs.pop(0) for _ in range(len(order) - 1 if last else 0)]
    grad_refs = [refs.pop(0) for _ in range(pair if last else 0)]
    zone_ref = refs.pop(0) if last else None
    values_ref, image_ref, *outs = refs[2 * slot :]
    rows = values_ref.shape[0] // 2
    part = slice(slot * rows, (slot + 1) * rows)
    fill(layers, width, pieces, top_ref, values_ref.at[part])
    image_layers(layers, width, values_ref.at[part], image_ref.at[part], matrix)
    found = products(held, values_ref, image_ref, slot)
    nodes = slice(0, 3 * layers * width)
    grad = product(force_ref[:, nodes], values_ref[:, nodes])[:8] if slot else None
    if not last:
        for j, value in enumerate(found):
            outs[0][j] = value
        if slot:
            outs[1][...] = grad
        return
    keep_ref, send_ref = outs
    half, blocks = rows // 2, len(order)
    pairs = [(i, j) for i in order for j in order]
    lay_out((keep_ref, send_ref), place, half, pairs, blocks_of(order, [*block_refs, found]))
    row = lax.broadcasted_iota(jnp.int32, (blocks, rows), 0)
    small = jnp.zeros((blocks, rows), jnp.float32)
    grads = [*(r[...] for r in grad_refs), grad]
    for j, name in enumerate(order):
        value = grads[j // 2][:1, j % 2 * rows : (j % 2 + 1) * rows]
        small = jnp.where(row == (place[0] ^ name), jnp.broadcast_to(value, (blocks, rows)), small)
    for j in range(blocks):
        columns = slice(j * rows, (j + 1) * rows)
        for ref in (keep_ref, send_ref):
            ref[blocks * half : blocks * half + blocks, columns] = small
            ref[blocks * half + blocks :, columns] = zone_ref[...]


def lay_out(refs, place, half, pairs, block):
    for i, j in pairs:
        at = pl.ds(pl.multiple_of((i ^ place[2]) * half, half), half)
        value = block(i, j)
        columns = slice(2 * half * j, 2 * half * (j + 1))
        refs[0][at, columns] = jnp.where(place[1] == 0, value[:half], value[half:])
        refs[1][at, columns] = jnp.where(place[1] == 0, value[half:], value[:half])


def blocks_of(order, block_refs):
    def block(i, j):
        first, second = order.index(i), order.index(j)
        value = block_refs[max(first, second)][min(first, second)]
        return value.T if first < second else value

    return block


def vmem_call(kernel, scalars, args, outs, scratch=(), aliases=None, name="image"):
    vmem = pl.BlockSpec(memory_space=pltpu.VMEM)
    return pl.pallas_call(
        kernel,
        in_specs=[pl.BlockSpec(memory_space=pltpu.SMEM)] * len(scalars) + [vmem] * len(args),
        out_specs=[vmem] * len(outs),
        out_shape=outs,
        scratch_shapes=list(scratch),
        input_output_aliases=aliases or {},
        compiler_params=pltpu.CompilerParams(vmem_limit_bytes=8 << 20),
        cost_estimate=pl.CostEstimate(flops=0, bytes_accessed=16 << 20, transcendentals=0),
        name=name,
    )(*scalars, *args)


def on_device(sensitivity, residual_force, moments, zone_label, misfit):
    cols = sensitivity.shape[1]
    layers = moments.shape[1]
    plane = GX * GY
    n_slab = lax.axis_size("slab")
    n_col = lax.axis_size("col")
    assert n_slab == 2 * n_col
    width = cols * n_col
    source = pltpu.with_memory_space_constraint(sensitivity, pltpu.HBM)
    lanes = plane // n_col
    bottom, total = 3 * lanes + EDGE, 3 * (layers + 1) * lanes + EDGE
    last = n_col - 1
    order = sorted(range(1, n_col), key=lambda k: (k.bit_count(), -k))
    single = [k for k in order if k.bit_count() == 1]
    double = [k for k in order if k.bit_count() > 1 and k != last]
    full = (0, cols)
    calls = [
        [(k, range(layers), full) for k in single],
        [(k, range(layers), full) for k in double]
        + [(last, range(layers // 2), full), (last, range(layers // 2, layers), full)]
        + [(0, range(1), full), (0, range(1, layers), full)],
    ]
    after, pieces = [], {}
    for specs in calls:
        packed, place = pack(source, after, specs, layers, plane, n_col)
        after = [place]
        for (k, _, _), array in zip(specs, packed):
            pieces.setdefault(k, []).append(exchange(array, "col", k) if k else array)
    *matrix, zone = build(moments, zone_label, misfit, residual_force, place, n_col, cols)
    held, blocks, grads, seen = [], [], [], []
    two = pltpu.VMEM((2 * cols, total), jnp.bfloat16)
    wide = pltpu.VMEM((width // 2 + 2 * n_col, width), jnp.float32)
    for k in (0, *order):
        low = crop(pieces[k][0], bottom, blocks[1 if k == last else 0]) if k else pieces[k][0]
        top = shifted(low, "slab", -1)
        slot = len(seen) % 2
        seen.append(k)
        args = [*pieces[k], top, *matrix, *(x for pair in held for x in pair)]
        outs = [two, two]
        if k == last:
            args += [*blocks, *grads, zone]
            outs += [wide, wide]
        else:
            outs.append(pltpu.VMEM((len(seen), cols, cols), jnp.float32))
            outs += [pltpu.VMEM((8, 2 * cols), jnp.float32)] * slot
        scalars, aliases = [place] * (k == last), {}
        if slot:
            aliases = {len(scalars) + len(args) + i: i for i in range(2)}
            args += current
        kernel = functools.partial(image_kernel, layers, lanes, len(pieces[k]), tuple(seen), k == last)
        out = vmem_call(kernel, scalars, args, outs, (), aliases)
        if k == last:
            keep, send = out[2:]
        else:
            out = [in_vmem(x) for x in out]
            current = out[:2]
            blocks.append(out[2])
            grads += out[3:]
            held += [current] * slot

    mine = keep + exchange(send, "slab", 1)
    parts = [mine[:, k * cols : (k + 1) * cols] for k in range(n_col)]
    mine = parts[0]
    for k in (order[0], *order[:0:-1]):
        mine = mine + exchange(parts[k], "col", k)
    half, rows = cols // 2, width // 2
    parts = [jnp.concatenate([mine[k * half : (k + 1) * half], mine[rows:]]) for k in range(n_col)]
    parts = [parts[0]] + [exchange(parts[k], "slab", 2 * k) for k in (1, *range(n_col - 1, 1, -1))]
    hessian = sum(part[:half] for part in parts).T
    both = sum(part[half:] for part in parts).reshape(2, width)
    gradient = both[0]
    zone_misfit = both[1] * (width / (layers * plane * n_slab))
    return (hessian, gradient, zone_misfit)


def solution(mesh):
    in_specs = (
        P(None, "col", "slab"),
        P(None, "slab"),
        P(None, "slab", None),
        P("slab", None),
        P("slab", None),
    )
    out_specs = (P("col", "slab"), P(), P())
    return jax.shard_map(
        on_device, mesh=mesh, in_specs=in_specs, out_specs=out_specs, check_vma=False
    )
```

```python
import functools

import jax
import jax.numpy as jnp
from jax import lax
from jax.experimental import pallas as pl
from jax.experimental.pallas import tpu as pltpu
from jax.sharding import PartitionSpec as P

GX = 64
GY = 16
TILE = 128
EDGE = 256


def exchange(value, axis, by):
    count = lax.axis_size(axis)
    return lax.ppermute(value, axis, [(i, i ^ by) for i in range(count)])


def shifted(value, axis, by):
    count = lax.axis_size(axis)
    pairs = [(i, i + by) for i in range(count) if 0 <= i + by < count]
    return lax.ppermute(value, axis, pairs)


def lane_of(shape):
    return lax.broadcasted_iota(jnp.int32, shape, 1)


def pack_kernel(layers, plane, n_col, specs, after, sens_ref, *refs):
    outs, (planes, sems) = refs[:-2], refs[-2:]
    col, slab = lax.axis_index("col"), lax.axis_index("slab")
    outs = list(outs)
    next_ref = outs.pop()
    outs = outs[after:]
    width = plane // n_col
    for i, value in enumerate((col, slab % 2, col ^ (slab // 2))):
        next_ref[i] = value
    inner, both = slice(0, width), slice(0, width + TILE)
    slots, waits = {}, {}
    for label in dict.fromkeys(spec[0] for spec in specs):
        spans = [levels for name, levels, _ in specs if name == label]
        edges = any(levels[0] == 0 for levels in spans)
        for level in range(layers):
            held = any(level in levels for levels in spans)
            if not (held or edges):
                continue
            target = col ^ label
            slot = slots[label, level] = len(slots)
            start = pl.multiple_of((level * n_col + target) * width, width)

            def copy(part, start=start, slot=slot):
                source = sens_ref.at[:, :, pl.ds(start + part.start, part.stop - part.start)]
                return pltpu.make_async_copy(source, planes.at[slot, :, :, part], sems.at[slot])

            inside = target != n_col - 1
            if not edges:
                cases = [(None, inner)]
            elif held:
                cases = [(inside, both), (jnp.logical_not(inside), inner)]
            else:
                cases = [(inside, slice(width, width + TILE))]
            for case, part in cases:
                if case is None:
                    copy(part).start()
                else:
                    pl.when(case)(copy(part).start)
            waits[label, level] = [(case, copy(part)) for case, part in cases]
    dtype = sens_ref.dtype
    for array, (label, levels, rows) in zip(outs, specs):
        lane = lane_of((rows[1] - rows[0], TILE))
        halo = [jnp.zeros(lane.shape, jnp.float32)] * (EDGE // TILE)
        start = 0
        for level in range(layers):
            if level not in levels and levels[0]:
                continue
            for case, copy in waits.pop((label, level), ()):
                if case is None:
                    copy.wait()
                else:
                    pl.when(case)(copy.wait)
            for k in range(3):
                piece = planes.at[slots[label, level], k, rows[0] : rows[1]]
                if level in levels:
                    array[:, start : start + width] = piece[:, inner]
                    start += width
                if levels[0] == 0:
                    tile, at = divmod(edge_at(k, level, layers), TILE)
                    edge = piece[:, width:].astype(jnp.float32)
                    edge = pltpu.roll(edge, at, 1) if at else edge
                    keep = (lane >= at) & (lane < at + GY) & ((col ^ label) != n_col - 1)
                    halo[tile] = jnp.where(keep, edge, halo[tile])
            if level == 0:
                start += EDGE
        if levels[0] == 0:
            for tile, value in enumerate(halo):
                begin = 3 * width + tile * TILE
                array[:, begin : begin + TILE] = value.astype(dtype)


def edge_at(k, level, layers):
    return (k * (layers + 1) + level) * GY


def pack(sensitivity, after, specs, layers, plane, n_col):
    cols, dtype = sensitivity.shape[1], sensitivity.dtype
    width = plane // n_col
    outs, slots = [], set()
    for label, levels, rows in specs:
        size = 3 * len(levels) * width + (0 if levels[0] else EDGE)
        outs.append(jax.ShapeDtypeStruct((rows[1] - rows[0], size), dtype))
        slots |= {(label, level) for level in (levels if levels[0] else range(layers))}
    *found, place = pl.pallas_call(
        functools.partial(pack_kernel, layers, plane, n_col, specs, len(after)),
        in_specs=[pl.BlockSpec(memory_space=pltpu.HBM)] + [pl.BlockSpec(memory_space=pltpu.SMEM)] * len(after),
        out_specs=[pl.BlockSpec(memory_space=pltpu.VMEM)] * len(outs) + [pl.BlockSpec(memory_space=pltpu.SMEM)],
        out_shape=[*outs, jax.ShapeDtypeStruct((3,), jnp.int32)],
        scratch_shapes=[
            pltpu.VMEM((len(slots), 3, cols, width + TILE), dtype),
            pltpu.SemaphoreType.DMA((len(slots),)),
        ],
        compiler_params=pltpu.CompilerParams(vmem_limit_bytes=8 << 20),
        cost_estimate=pl.CostEstimate(flops=0, bytes_accessed=4 << 20, transcendentals=0),
        name="pack",
    )(sensitivity, *after)
    return found, place


def crop_kernel(piece_ref, _, out_ref):
    out_ref[...] = piece_ref[:, : out_ref.shape[1]]


def crop(piece, size, after):
    return pl.pallas_call(
        crop_kernel,
        in_specs=[pl.BlockSpec(memory_space=pltpu.VMEM), pl.BlockSpec(memory_space=pl.ANY)],
        out_specs=pl.BlockSpec(memory_space=pltpu.VMEM),
        out_shape=jax.ShapeDtypeStruct((piece.shape[0], size), piece.dtype),
        compiler_params=pltpu.CompilerParams(vmem_limit_bytes=8 << 20),
        cost_estimate=pl.CostEstimate(flops=0, bytes_accessed=0, transcendentals=0),
        name="crop",
    )(piece, after)


def component(a, b):
    a, b = min(a, b), max(a, b)
    return a if a == b else a + b + 2


def tile_start(z, k, side, other, layers):
    base = 15 * z + ((0, 6, 11)[k] if z < layers else (0, 3, 5)[k])
    return base + (other - k if side == 0 else 3 - k + other)


def zone_sums(label_ref, misfit_ref, zone_ref):
    f32, bf16 = jnp.float32, jnp.bfloat16
    layers, width = label_ref.shape
    blocks, cols = zone_ref.shape
    row = lax.broadcasted_iota(jnp.int32, (8, width), 0)
    zone = lax.broadcasted_iota(jnp.int32, (cols, width), 0)
    for b in range(blocks):
        total = jnp.zeros((8, cols), f32)
        for level in range(layers):
            value = jnp.broadcast_to(misfit_ref[level : level + 1], (8, width))
            high = value.astype(bf16).astype(f32)
            middle = (value - high).astype(bf16).astype(f32)
            low = value - high - middle
            terms = jnp.where(row == 0, high, jnp.where(row == 1, middle, jnp.where(row == 2, low, 0.0)))
            label = jnp.broadcast_to(label_ref[level : level + 1], (cols, width))
            chosen = jnp.where(label == zone + b * cols, 1.0, 0.0).astype(bf16)
            total += lax.dot_general(
                terms.astype(bf16), chosen, (((1,), (1,)), ((), ())), preferred_element_type=f32
            )
        zone_ref[b : b + 1] = jnp.sum(total, axis=0, keepdims=True)


def build_kernel(layers, width, place, moments_ref, label_ref, misfit_ref, *refs):
    force_refs, refs = refs[:layers], refs[layers:]
    plane_ref, edge_ref, corner_ref, force_ref, zone_ref, field_ref, ahead_ref = refs
    f32, bf16 = jnp.float32, jnp.bfloat16
    force_ref[...] = jnp.zeros_like(force_ref)
    for z in range(layers):
        for k in range(3):
            value = force_refs[z][k : k + 1].astype(f32)
            start = (3 * z + k) * width
            force_ref[:, start : start + width] = jnp.broadcast_to(value, (16, width)).astype(bf16)
    zone_sums(label_ref, misfit_ref, zone_ref)
    shape = (GY, width)
    lane = lane_of(shape)
    row = lax.broadcasted_iota(jnp.int32, shape, 0)
    pos_x, pos_y = lane // GY, lane % GY
    same, up, down = row == pos_y, row == pos_y + 1, row == pos_y - 1
    zero = jnp.zeros(shape, f32)
    field_lane = lane_of((8, width))
    columns = width // GY
    near = [pos_x % 3 == r for r in range(3)]
    follow = [(pos_x + 1) % 3 == r for r in range(3)]
    band = [jnp.where((pos_x >= x - 1) & (pos_x <= x + 1), 1.0, 0.0).astype(bf16) for x in range(columns)]
    tile_lane = lane_of((GY, TILE))

    def spread(middle, ahead, behind):
        def whole(value):
            return jnp.broadcast_to(value, shape)

        return jnp.where(same, whole(middle), jnp.where(up, whole(ahead), jnp.where(down, whole(behind), zero)))

    def two_terms(value):
        hi = value.astype(bf16)
        return hi, (value - hi.astype(f32)).astype(bf16)

    edge_ref[...] = jnp.zeros_like(edge_ref)
    field_ref[...] = jnp.zeros_like(field_ref)
    for z in range(layers + 1):
        whole = None
        for level in (z, z - 1):
            if 0 <= level < layers:
                part = moments_ref[:, level, :] * (2.0 / 216.0)
                whole = part if whole is None else whole + part
        field_ref[2 * z, :6] = whole
        if z < layers:
            field_ref[2 * z + 1, :6] = moments_ref[:, z, :] * (1.0 / 216.0)

    for pair in range(2 * layers + 1):
        z, side = divmod(pair, 2)
        element = field_ref[pair]
        before = jnp.where(field_lane >= GY, pltpu.roll(element, GY, 1), 0.0)
        parts = []
        for value in (2.0 * (element + before), element, before):
            lower = jnp.where(field_lane % GY != 0, pltpu.roll(value, 1, 1), 0.0)
            parts.append((2.0 * (value + lower), value, lower))
        for c in range(6):
            here, ahead, behind = [spread(*(v[c : c + 1] for v in part)) for part in parts]
            ahead_ref[pair, c] = ahead[:, width - TILE :]
            scale = 0.5 if side == 0 and c < 3 else None
            spots = []
            for k in range(3):
                for other in range(3):
                    if component(k, other) == c and (side == 1 or other >= k):
                        spots.append(tile_start(z, k, side, other, layers))
            for r in range(3):
                value = jnp.where(near[r], here, jnp.where(follow[r], ahead, behind))
                if scale is not None:
                    value = value * scale
                for term, piece in enumerate(two_terms(value)):
                    for x in range(r, columns, 3):
                        block = piece * band[x]
                        for spot in spots:
                            start = spot * width + x * GY
                            plane_ref[term, start : start + GY, :] = block

    edge_lane = tile_lane // GY == TILE // GY - 1
    for z in range(layers + 1):
        for other_z in range(max(z - 1, 0), min(z + 1, layers) + 1):
            pair = 2 * z if other_z == z else 2 * min(z, other_z) + 1
            for c in range(6):
                value = jnp.where(edge_lane, ahead_ref[pair, c], 0.0)
                for term, piece in enumerate(two_terms(value)):
                    for k in range(3):
                        for other in range(3):
                            if component(k, other) == c:
                                start = edge_at(other, other_z, layers)
                                n, at = divmod(3 * z + k, 2)
                                edge_ref[term, n, start : start + GY, at * TILE : (at + 1) * TILE] = piece

    corner_ref[...] = jnp.zeros_like(corner_ref)
    for other_z in range(layers + 1):
        for other in range(3):
            tiles = [jnp.zeros((GY, TILE), f32)] * (EDGE // TILE)
            for z in range(max(other_z - 1, 0), min(other_z + 1, layers) + 1):
                pair = 2 * z if other_z == z else 2 * min(z, other_z) + 1
                for k in range(3):
                    tile, at = divmod(edge_at(k, z, layers), TILE)
                    value = ahead_ref[pair, component(k, other)]
                    turn = (at + GY) % TILE
                    value = pltpu.roll(value, turn, 1) if turn else value
                    tiles[tile] = jnp.where(tile_lane // GY == at // GY, value, tiles[tile])
            start = edge_at(other, other_z, layers)
            for tile, value in enumerate(tiles):
                for term, piece in enumerate(two_terms(value)):
                    corner_ref[term, start : start + GY, tile * TILE : (tile + 1) * TILE] = piece


def in_vmem(x):
    return pltpu.with_memory_space_constraint(x, pltpu.VMEM)


def build(moments, zone_label, misfit, residual_force, place, n_col, cols):
    layers, plane = zone_label.shape
    width = plane // n_col
    shapes = [
        ((2, (15 * layers + 6) * width, width), jnp.bfloat16),
        ((2, (3 * layers + 4) // 2, EDGE, 2 * TILE), jnp.bfloat16),
        ((2, EDGE, EDGE), jnp.bfloat16),
        ((16, 3 * (layers + 1) * width + EDGE), jnp.bfloat16),
        ((n_col, cols), jnp.float32),
    ]

    def force_spec(level):
        return pl.BlockSpec((3, width), lambda i, t: (0, level * n_col + t[0]))

    out = pl.pallas_call(
        functools.partial(build_kernel, layers, width),
        grid_spec=pltpu.PrefetchScalarGridSpec(
            num_scalar_prefetch=1,
            grid=(1,),
            in_specs=[
                pl.BlockSpec((6, layers, width), lambda i, t: (0, 0, t[0])),
                pl.BlockSpec((layers, width), lambda i, t: (0, t[0])),
                pl.BlockSpec((layers, width), lambda i, t: (0, t[0])),
            ]
            + [force_spec(level) for level in range(layers)],
            out_specs=[pl.BlockSpec(memory_space=pltpu.VMEM)] * len(shapes),
            scratch_shapes=[
                pltpu.VMEM((2 * layers + 1, 8, width), jnp.float32),
                pltpu.VMEM((2 * layers + 1, 6, GY, TILE), jnp.float32),
            ],
        ),
        out_shape=[pltpu.VMEM(*shape) for shape in shapes],
        compiler_params=pltpu.CompilerParams(vmem_limit_bytes=8 << 20),
        cost_estimate=pl.CostEstimate(flops=0, bytes_accessed=12 << 20, transcendentals=0),
        name="build",
    )(place, moments, zone_label, misfit, *([residual_force] * layers))
    return [in_vmem(x) for x in out]


def image_layers(layers, width, values_ref, image_ref, matrix):
    plane_ref, edge_ref, corner_ref = matrix
    f32, bf16 = jnp.float32, jnp.bfloat16
    depth = 3 * (layers + 1) * width
    halo = values_ref[:, depth:]

    def dot(a, b):
        return jnp.dot(a, b, preferred_element_type=f32)

    edges = []
    for n in range(edge_ref.shape[1]):
        both = dot(halo, edge_ref[0, n]) + dot(halo, edge_ref[1, n])
        edges += [both[:, :TILE], both[:, TILE:]]
    for z in range(layers + 1):
        for k in range(3):
            lo = (3 * z + k) * width
            hi = min(3 * (z + 2) * width, depth)
            start = tile_start(z, k, 0, k, layers) * width
            value, held = values_ref[:, lo:hi], plane_ref.at[:, start : start + hi - lo, :]
            total = dot(value, held[0]) + dot(value, held[1])
            inner = width - TILE
            if inner:
                image_ref[:, lo : lo + inner] = total[:, :inner].astype(bf16)
            image_ref[:, lo + inner : lo + width] = (total[:, inner:] + edges[3 * z + k]).astype(bf16)
    image_ref[:, depth:] = (dot(halo, corner_ref[0]) + dot(halo, corner_ref[1])).astype(bf16)


def copy_in(pieces, start, values_ref, width):
    for array in pieces:
        if start == 0:
            values_ref[:, : 3 * width] = array[:, : 3 * width]
            start, skip = 3 * width, 3 * width + EDGE
        else:
            skip = 0
        if skip < array.shape[1]:
            end = start + array.shape[1] - skip
            values_ref[:, start:end] = array[:, skip:]
            start = end


def halo_of(first_ref, top_ref, layers, width):
    group = lane_of((first_ref.shape[0], EDGE)) // GY
    halo = first_ref[:, 3 * width : 3 * width + EDGE].astype(jnp.float32)
    top = pltpu.roll(top_ref[:, 3 * width :].astype(jnp.float32), layers * GY, 1)
    halo = jnp.where(group % (layers + 1) == layers, top, halo)
    return jnp.where(group < 3 * (layers + 1), halo, 0.0).astype(jnp.bfloat16)


def product(a, b):
    return lax.dot_general(a, b, (((1,), (1,)), ((), ())), preferred_element_type=jnp.float32)


def products(held, values_ref, image_ref, slot):
    rows = values_ref.shape[0] // 2
    value, image = (ref[slot * rows : (slot + 1) * rows] for ref in (values_ref, image_ref))
    found = []
    for v, i in held:
        both = jnp.dot(image, v[...], preferred_element_type=jnp.float32)
        both += jnp.dot(value, i[...], preferred_element_type=jnp.float32)
        found += [both[:, :rows], both[:, rows:]]
    if slot:
        both = product(image, values_ref[...])
        found.append(both[:, :rows] + product(value, image_ref[:rows]))
        own = both[:, rows:]
    else:
        own = product(image, value)
    return [*found, own + own.T]


def fill(layers, width, pieces, top_ref, values_ref):
    depth = 3 * (layers + 1) * width
    copy_in(pieces, 0, values_ref, width)
    values_ref[:, 3 * layers * width : depth] = top_ref[:, : 3 * width]
    values_ref[:, depth:] = halo_of(pieces[0], top_ref, layers, width)


def image_kernel(layers, width, arrays, order, last, turn, *refs):
    refs, (pair, slot) = list(refs), divmod(len(order) - 1, 2)
    place = refs.pop(0) if last else None
    pieces = [refs.pop(0) for _ in range(arrays)]
    top_ref, *matrix, force_ref = (refs.pop(0) for _ in range(5))
    held = [(refs.pop(0), refs.pop(0)) for _ in range(pair)]
    block_refs = [refs.pop(0) for _ in range(len(order) - 1 if last else 0)]
    grad_refs = [refs.pop(0) for _ in range(pair if last else 0)]
    zone_ref = refs.pop(0) if last else None
    values_ref, image_ref, *outs = refs[(4 if turn else 2) * slot :]
    rows = values_ref.shape[0] // 2
    part = slice(slot * rows, (slot + 1) * rows)
    fill(layers, width, pieces, top_ref, values_ref.at[part])
    image_layers(layers, width, values_ref.at[part], image_ref.at[part], matrix)
    found = products(held, values_ref, image_ref, slot)
    nodes = slice(0, 3 * layers * width)
    grad = product(force_ref[:, nodes], values_ref[:, nodes])[:8] if slot else None
    if not last:
        if turn:
            turned, outs = outs[:2], outs[2:]
            step = min(2 * TILE, width)
            for start in range(0, values_ref.shape[1], step):
                for ref, to in zip((values_ref, image_ref), turned):
                    to[start : start + step, part] = ref[part, start : start + step].T
        for j, value in enumerate(found):
            outs[0][j] = value
        if slot:
            outs[1][...] = grad
        return
    keep_ref, send_ref = outs
    half, blocks = rows // 2, len(order)
    pairs = [(i, j) for i in order for j in order]
    lay_out((keep_ref, send_ref), place, half, pairs, blocks_of(order, [*block_refs, found]))
    row = lax.broadcasted_iota(jnp.int32, (blocks, rows), 0)
    small = jnp.zeros((blocks, rows), jnp.float32)
    grads = [*(r[...] for r in grad_refs), grad]
    for j, name in enumerate(order):
        value = grads[j // 2][:1, j % 2 * rows : (j % 2 + 1) * rows]
        small = jnp.where(row == (place[0] ^ name), jnp.broadcast_to(value, (blocks, rows)), small)
    for j in range(blocks):
        columns = slice(j * rows, (j + 1) * rows)
        for ref in (keep_ref, send_ref):
            ref[blocks * half : blocks * half + blocks, columns] = small
            ref[blocks * half + blocks :, columns] = zone_ref[...]


def lay_out(refs, place, half, pairs, block):
    for i, j in pairs:
        at = pl.ds(pl.multiple_of((i ^ place[2]) * half, half), half)
        value = block(i, j)
        columns = slice(2 * half * j, 2 * half * (j + 1))
        refs[0][at, columns] = jnp.where(place[1] == 0, value[:half], value[half:])
        refs[1][at, columns] = jnp.where(place[1] == 0, value[half:], value[:half])


def blocks_of(order, block_refs):
    def block(i, j):
        first, second = order.index(i), order.index(j)
        value = block_refs[max(first, second)][min(first, second)]
        return value.T if first < second else value

    return block


def vmem_call(kernel, scalars, args, outs, scratch=(), aliases=None, name="image"):
    vmem = pl.BlockSpec(memory_space=pltpu.VMEM)
    return pl.pallas_call(
        kernel,
        in_specs=[pl.BlockSpec(memory_space=pltpu.SMEM)] * len(scalars) + [vmem] * len(args),
        out_specs=[vmem] * len(outs),
        out_shape=outs,
        scratch_shapes=list(scratch),
        input_output_aliases=aliases or {},
        compiler_params=pltpu.CompilerParams(vmem_limit_bytes=8 << 20),
        cost_estimate=pl.CostEstimate(flops=0, bytes_accessed=16 << 20, transcendentals=0),
        name=name,
    )(*scalars, *args)


def on_device(sensitivity, residual_force, moments, zone_label, misfit):
    cols = sensitivity.shape[1]
    layers = moments.shape[1]
    plane = GX * GY
    n_slab = lax.axis_size("slab")
    n_col = lax.axis_size("col")
    assert n_slab == 2 * n_col
    width = cols * n_col
    source = pltpu.with_memory_space_constraint(sensitivity, pltpu.HBM)
    lanes = plane // n_col
    bottom, total = 3 * lanes + EDGE, 3 * (layers + 1) * lanes + EDGE
    last = n_col - 1
    order = sorted(range(1, n_col), key=lambda k: (k.bit_count(), -k))
    single = [k for k in order if k.bit_count() == 1]
    double = [k for k in order if k.bit_count() > 1 and k != last]
    full = (0, cols)
    calls = [
        [(k, range(layers), full) for k in single],
        [(k, range(layers), full) for k in double]
        + [(last, range(layers // 2), full), (last, range(layers // 2, layers), full)]
        + [(0, range(1), full), (0, range(1, layers), full)],
    ]
    after, pieces = [], {}
    for specs in calls:
        packed, place = pack(source, after, specs, layers, plane, n_col)
        after = [place]
        for (k, _, _), array in zip(specs, packed):
            pieces.setdefault(k, []).append(exchange(array, "col", k) if k else array)
    *matrix, zone = build(moments, zone_label, misfit, residual_force, place, n_col, cols)
    held, blocks, grads, seen = [], [], [], []
    two = pltpu.VMEM((2 * cols, total), jnp.bfloat16)
    wide = pltpu.VMEM((width // 2 + 2 * n_col, width), jnp.float32)
    for k in (0, *order):
        low = crop(pieces[k][0], bottom, blocks[1 if k == last else 0]) if k else pieces[k][0]
        top = shifted(low, "slab", -1)
        slot = len(seen) % 2
        seen.append(k)
        args = [*pieces[k], top, *matrix, *(x for pair in held for x in pair)]
        outs = [two, two]
        if len(seen) <= n_col - 2:
            outs += [pltpu.VMEM((total, 2 * cols), jnp.bfloat16)] * 2
        count = len(outs)
        if k == last:
            args += [*blocks, *grads, zone]
            outs += [wide, wide]
        else:
            outs.append(pltpu.VMEM((len(seen), cols, cols), jnp.float32))
            outs += [pltpu.VMEM((8, 2 * cols), jnp.float32)] * slot
        scalars, aliases = [place] * (k == last), {}
        if slot:
            aliases = {len(scalars) + len(args) + i: i for i in range(count)}
            args += current
        kernel = functools.partial(image_kernel, layers, lanes, len(pieces[k]), tuple(seen), k == last, count > 2)
        out = vmem_call(kernel, scalars, args, outs, (), aliases)
        if k == last:
            keep, send = out[2:]
        else:
            out = [in_vmem(x) for x in out]
            current = out[:count]
            blocks.append(out[count])
            grads += out[count + 1 :]
            held += [current[2:]] * slot

    mine = keep + exchange(send, "slab", 1)
    parts = [mine[:, k * cols : (k + 1) * cols] for k in range(n_col)]
    mine = parts[0]
    for k in range(1, n_col):
        mine = mine + exchange(parts[k], "col", k)
    half, rows = cols // 2, width // 2
    parts = [jnp.concatenate([mine[k * half : (k + 1) * half], mine[rows:]]) for k in range(n_col)]
    parts = [parts[0]] + [exchange(parts[k], "slab", 2 * k) for k in range(1, n_col)]
    hessian = sum(part[:half] for part in parts).T
    both = sum(part[half:] for part in parts).reshape(2, width)
    gradient = both[0]
    zone_misfit = both[1] * (width / (layers * plane * n_slab))
    return (hessian, gradient, zone_misfit)


def solution(mesh):
    in_specs = (
        P(None, "col", "slab"),
        P(None, "slab"),
        P(None, "slab", None),
        P("slab", None),
        P("slab", None),
    )
    out_specs = (P("col", "slab"), P(), P())
    return jax.shard_map(
        on_device, mesh=mesh, in_specs=in_specs, out_specs=out_specs, check_vma=False
    )
```

```python
import functools

import jax
import jax.numpy as jnp
from jax import lax
from jax.experimental import pallas as pl
from jax.experimental.pallas import tpu as pltpu
from jax.sharding import PartitionSpec as P

GX = 64
GY = 16
TILE = 128
EDGE = 256


def exchange(value, axis, by):
    count = lax.axis_size(axis)
    return lax.ppermute(value, axis, [(i, i ^ by) for i in range(count)])


def shifted(value, axis, by):
    count = lax.axis_size(axis)
    pairs = [(i, i + by) for i in range(count) if 0 <= i + by < count]
    return lax.ppermute(value, axis, pairs)


def lane_of(shape):
    return lax.broadcasted_iota(jnp.int32, shape, 1)


def pack_kernel(layers, plane, n_col, specs, after, sens_ref, *refs):
    outs, (planes, sems) = refs[:-2], refs[-2:]
    col, slab = lax.axis_index("col"), lax.axis_index("slab")
    outs = list(outs)
    next_ref = outs.pop()
    outs = outs[after:]
    width = plane // n_col
    for i, value in enumerate((col, slab % 2, col ^ (slab // 2))):
        next_ref[i] = value
    inner, both = slice(0, width), slice(0, width + TILE)
    slots, waits = {}, {}
    for label in dict.fromkeys(spec[0] for spec in specs):
        spans = [levels for name, levels, _ in specs if name == label]
        edges = any(levels[0] == 0 for levels in spans)
        for level in range(layers):
            held = any(level in levels for levels in spans)
            if not (held or edges):
                continue
            target = col ^ label
            slot = slots[label, level] = len(slots)
            start = pl.multiple_of((level * n_col + target) * width, width)

            def copy(part, start=start, slot=slot):
                source = sens_ref.at[:, :, pl.ds(start + part.start, part.stop - part.start)]
                return pltpu.make_async_copy(source, planes.at[slot, :, :, part], sems.at[slot])

            inside = target != n_col - 1
            if not edges:
                cases = [(None, inner)]
            elif held:
                cases = [(inside, both), (jnp.logical_not(inside), inner)]
            else:
                cases = [(inside, slice(width, width + TILE))]
            for case, part in cases:
                if case is None:
                    copy(part).start()
                else:
                    pl.when(case)(copy(part).start)
            waits[label, level] = [(case, copy(part)) for case, part in cases]
    dtype = sens_ref.dtype
    for array, (label, levels, rows) in zip(outs, specs):
        lane = lane_of((rows[1] - rows[0], TILE))
        halo = [jnp.zeros(lane.shape, jnp.float32)] * (EDGE // TILE)
        start = 0
        for level in range(layers):
            if level not in levels and levels[0]:
                continue
            for case, copy in waits.pop((label, level), ()):
                if case is None:
                    copy.wait()
                else:
                    pl.when(case)(copy.wait)
            for k in range(3):
                piece = planes.at[slots[label, level], k, rows[0] : rows[1]]
                if level in levels:
                    array[:, start : start + width] = piece[:, inner]
                    start += width
                if levels[0] == 0:
                    tile, at = divmod(edge_at(k, level, layers), TILE)
                    edge = piece[:, width:].astype(jnp.float32)
                    edge = pltpu.roll(edge, at, 1) if at else edge
                    keep = (lane >= at) & (lane < at + GY) & ((col ^ label) != n_col - 1)
                    halo[tile] = jnp.where(keep, edge, halo[tile])
            if level == 0:
                start += EDGE
        if levels[0] == 0:
            for tile, value in enumerate(halo):
                begin = 3 * width + tile * TILE
                array[:, begin : begin + TILE] = value.astype(dtype)


def edge_at(k, level, layers):
    return (k * (layers + 1) + level) * GY


def pack(sensitivity, after, specs, layers, plane, n_col):
    cols, dtype = sensitivity.shape[1], sensitivity.dtype
    width = plane // n_col
    outs, slots = [], set()
    for label, levels, rows in specs:
        size = 3 * len(levels) * width + (0 if levels[0] else EDGE)
        outs.append(jax.ShapeDtypeStruct((rows[1] - rows[0], size), dtype))
        slots |= {(label, level) for level in (levels if levels[0] else range(layers))}
    *found, place = pl.pallas_call(
        functools.partial(pack_kernel, layers, plane, n_col, specs, len(after)),
        in_specs=[pl.BlockSpec(memory_space=pltpu.HBM)] + [pl.BlockSpec(memory_space=pltpu.SMEM)] * len(after),
        out_specs=[pl.BlockSpec(memory_space=pltpu.VMEM)] * len(outs) + [pl.BlockSpec(memory_space=pltpu.SMEM)],
        out_shape=[*outs, jax.ShapeDtypeStruct((3,), jnp.int32)],
        scratch_shapes=[
            pltpu.VMEM((len(slots), 3, cols, width + TILE), dtype),
            pltpu.SemaphoreType.DMA((len(slots),)),
        ],
        compiler_params=pltpu.CompilerParams(vmem_limit_bytes=8 << 20),
        cost_estimate=pl.CostEstimate(flops=0, bytes_accessed=4 << 20, transcendentals=0),
        name="pack",
    )(sensitivity, *after)
    return found, place


def crop_kernel(piece_ref, _, out_ref):
    out_ref[...] = piece_ref[:, : out_ref.shape[1]]


def crop(piece, size, after):
    return pl.pallas_call(
        crop_kernel,
        in_specs=[pl.BlockSpec(memory_space=pltpu.VMEM), pl.BlockSpec(memory_space=pl.ANY)],
        out_specs=pl.BlockSpec(memory_space=pltpu.VMEM),
        out_shape=jax.ShapeDtypeStruct((piece.shape[0], size), piece.dtype),
        compiler_params=pltpu.CompilerParams(vmem_limit_bytes=8 << 20),
        cost_estimate=pl.CostEstimate(flops=0, bytes_accessed=0, transcendentals=0),
        name="crop",
    )(piece, after)


def component(a, b):
    a, b = min(a, b), max(a, b)
    return a if a == b else a + b + 2


def tile_start(z, k, side, other, layers):
    base = 15 * z + ((0, 6, 11)[k] if z < layers else (0, 3, 5)[k])
    return base + (other - k if side == 0 else 3 - k + other)


def zone_sums(label_ref, misfit_ref, zone_ref):
    f32, bf16 = jnp.float32, jnp.bfloat16
    layers, width = label_ref.shape
    blocks, cols = zone_ref.shape
    row = lax.broadcasted_iota(jnp.int32, (8, width), 0)
    zone = lax.broadcasted_iota(jnp.int32, (cols, width), 0)
    for b in range(blocks):
        total = jnp.zeros((8, cols), f32)
        for level in range(layers):
            value = jnp.broadcast_to(misfit_ref[level : level + 1], (8, width))
            high = value.astype(bf16).astype(f32)
            middle = (value - high).astype(bf16).astype(f32)
            low = value - high - middle
            terms = jnp.where(row == 0, high, jnp.where(row == 1, middle, jnp.where(row == 2, low, 0.0)))
            label = jnp.broadcast_to(label_ref[level : level + 1], (cols, width))
            chosen = jnp.where(label == zone + b * cols, 1.0, 0.0).astype(bf16)
            total += lax.dot_general(
                terms.astype(bf16), chosen, (((1,), (1,)), ((), ())), preferred_element_type=f32
            )
        zone_ref[b : b + 1] = jnp.sum(total, axis=0, keepdims=True)


def build_kernel(layers, width, place, moments_ref, label_ref, misfit_ref, *refs):
    force_refs, refs = refs[:layers], refs[layers:]
    plane_ref, edge_ref, corner_ref, force_ref, zone_ref, field_ref, ahead_ref = refs
    f32, bf16 = jnp.float32, jnp.bfloat16
    force_ref[...] = jnp.zeros_like(force_ref)
    for z in range(layers):
        for k in range(3):
            value = force_refs[z][k : k + 1].astype(f32)
            start = (3 * z + k) * width
            force_ref[:, start : start + width] = jnp.broadcast_to(value, (16, width)).astype(bf16)
    zone_sums(label_ref, misfit_ref, zone_ref)
    shape = (GY, width)
    lane = lane_of(shape)
    row = lax.broadcasted_iota(jnp.int32, shape, 0)
    pos_x, pos_y = lane // GY, lane % GY
    same, up, down = row == pos_y, row == pos_y + 1, row == pos_y - 1
    zero = jnp.zeros(shape, f32)
    field_lane = lane_of((8, width))
    columns = width // GY
    near = [pos_x % 3 == r for r in range(3)]
    follow = [(pos_x + 1) % 3 == r for r in range(3)]
    band = [jnp.where((pos_x >= x - 1) & (pos_x <= x + 1), 1.0, 0.0).astype(bf16) for x in range(columns)]
    tile_lane = lane_of((GY, TILE))

    def spread(middle, ahead, behind):
        def whole(value):
            return jnp.broadcast_to(value, shape)

        return jnp.where(same, whole(middle), jnp.where(up, whole(ahead), jnp.where(down, whole(behind), zero)))

    def two_terms(value):
        hi = value.astype(bf16)
        return hi, (value - hi.astype(f32)).astype(bf16)

    edge_ref[...] = jnp.zeros_like(edge_ref)
    field_ref[...] = jnp.zeros_like(field_ref)
    for z in range(layers + 1):
        whole = None
        for level in (z, z - 1):
            if 0 <= level < layers:
                part = moments_ref[:, level, :] * (2.0 / 216.0)
                whole = part if whole is None else whole + part
        field_ref[2 * z, :6] = whole
        if z < layers:
            field_ref[2 * z + 1, :6] = moments_ref[:, z, :] * (1.0 / 216.0)

    for pair in range(2 * layers + 1):
        z, side = divmod(pair, 2)
        element = field_ref[pair]
        before = jnp.where(field_lane >= GY, pltpu.roll(element, GY, 1), 0.0)
        parts = []
        for value in (2.0 * (element + before), element, before):
            lower = jnp.where(field_lane % GY != 0, pltpu.roll(value, 1, 1), 0.0)
            parts.append((2.0 * (value + lower), value, lower))
        for c in range(6):
            here, ahead, behind = [spread(*(v[c : c + 1] for v in part)) for part in parts]
            ahead_ref[pair, c] = ahead[:, width - TILE :]
            scale = 0.5 if side == 0 and c < 3 else None
            spots = []
            for k in range(3):
                for other in range(3):
                    if component(k, other) == c and (side == 1 or other >= k):
                        spots.append(tile_start(z, k, side, other, layers))
            for r in range(3):
                value = jnp.where(near[r], here, jnp.where(follow[r], ahead, behind))
                if scale is not None:
                    value = value * scale
                for term, piece in enumerate(two_terms(value)):
                    for x in range(r, columns, 3):
                        block = piece * band[x]
                        for spot in spots:
                            start = spot * width + x * GY
                            plane_ref[term, start : start + GY, :] = block

    edge_lane = tile_lane // GY == TILE // GY - 1
    for z in range(layers + 1):
        for other_z in range(max(z - 1, 0), min(z + 1, layers) + 1):
            pair = 2 * z if other_z == z else 2 * min(z, other_z) + 1
            for c in range(6):
                value = jnp.where(edge_lane, ahead_ref[pair, c], 0.0)
                for term, piece in enumerate(two_terms(value)):
                    for k in range(3):
                        for other in range(3):
                            if component(k, other) == c:
                                start = edge_at(other, other_z, layers)
                                n, at = divmod(3 * z + k, 2)
                                edge_ref[term, n, start : start + GY, at * TILE : (at + 1) * TILE] = piece

    corner_ref[...] = jnp.zeros_like(corner_ref)
    for other_z in range(layers + 1):
        for other in range(3):
            tiles = [jnp.zeros((GY, TILE), f32)] * (EDGE // TILE)
            for z in range(max(other_z - 1, 0), min(other_z + 1, layers) + 1):
                pair = 2 * z if other_z == z else 2 * min(z, other_z) + 1
                for k in range(3):
                    tile, at = divmod(edge_at(k, z, layers), TILE)
                    value = ahead_ref[pair, component(k, other)]
                    turn = (at + GY) % TILE
                    value = pltpu.roll(value, turn, 1) if turn else value
                    tiles[tile] = jnp.where(tile_lane // GY == at // GY, value, tiles[tile])
            start = edge_at(other, other_z, layers)
            for tile, value in enumerate(tiles):
                for term, piece in enumerate(two_terms(value)):
                    corner_ref[term, start : start + GY, tile * TILE : (tile + 1) * TILE] = piece


def in_vmem(x):
    return pltpu.with_memory_space_constraint(x, pltpu.VMEM)


def build(moments, zone_label, misfit, residual_force, place, n_col, cols):
    layers, plane = zone_label.shape
    width = plane // n_col
    shapes = [
        ((2, (15 * layers + 6) * width, width), jnp.bfloat16),
        ((2, (3 * layers + 4) // 2, EDGE, 2 * TILE), jnp.bfloat16),
        ((2, EDGE, EDGE), jnp.bfloat16),
        ((16, 3 * (layers + 1) * width + EDGE), jnp.bfloat16),
        ((n_col, cols), jnp.float32),
    ]

    def force_spec(level):
        return pl.BlockSpec((3, width), lambda i, t: (0, level * n_col + t[0]))

    out = pl.pallas_call(
        functools.partial(build_kernel, layers, width),
        grid_spec=pltpu.PrefetchScalarGridSpec(
            num_scalar_prefetch=1,
            grid=(1,),
            in_specs=[
                pl.BlockSpec((6, layers, width), lambda i, t: (0, 0, t[0])),
                pl.BlockSpec((layers, width), lambda i, t: (0, t[0])),
                pl.BlockSpec((layers, width), lambda i, t: (0, t[0])),
            ]
            + [force_spec(level) for level in range(layers)],
            out_specs=[pl.BlockSpec(memory_space=pltpu.VMEM)] * len(shapes),
            scratch_shapes=[
                pltpu.VMEM((2 * layers + 1, 8, width), jnp.float32),
                pltpu.VMEM((2 * layers + 1, 6, GY, TILE), jnp.float32),
            ],
        ),
        out_shape=[pltpu.VMEM(*shape) for shape in shapes],
        compiler_params=pltpu.CompilerParams(vmem_limit_bytes=8 << 20),
        cost_estimate=pl.CostEstimate(flops=0, bytes_accessed=12 << 20, transcendentals=0),
        name="build",
    )(place, moments, zone_label, misfit, *([residual_force] * layers))
    return [in_vmem(x) for x in out]


def image_layers(layers, width, values_ref, image_ref, matrix):
    plane_ref, edge_ref, corner_ref = matrix
    f32, bf16 = jnp.float32, jnp.bfloat16
    depth = 3 * (layers + 1) * width
    halo = values_ref[:, depth:]

    def dot(a, b):
        return jnp.dot(a, b, preferred_element_type=f32)

    edges = []
    for n in range(edge_ref.shape[1]):
        both = dot(halo, edge_ref[0, n]) + dot(halo, edge_ref[1, n])
        edges += [both[:, :TILE], both[:, TILE:]]
    for z in range(layers + 1):
        for k in range(3):
            lo = (3 * z + k) * width
            hi = min(3 * (z + 2) * width, depth)
            start = tile_start(z, k, 0, k, layers) * width
            value, held = values_ref[:, lo:hi], plane_ref.at[:, start : start + hi - lo, :]
            total = dot(value, held[0]) + dot(value, held[1])
            inner = width - TILE
            if inner:
                image_ref[:, lo : lo + inner] = total[:, :inner].astype(bf16)
            image_ref[:, lo + inner : lo + width] = (total[:, inner:] + edges[3 * z + k]).astype(bf16)
    image_ref[:, depth:] = (dot(halo, corner_ref[0]) + dot(halo, corner_ref[1])).astype(bf16)


def copy_in(pieces, start, values_ref, width):
    for array in pieces:
        if start == 0:
            values_ref[:, : 3 * width] = array[:, : 3 * width]
            start, skip = 3 * width, 3 * width + EDGE
        else:
            skip = 0
        if skip < array.shape[1]:
            end = start + array.shape[1] - skip
            values_ref[:, start:end] = array[:, skip:]
            start = end


def halo_of(first_ref, top_ref, layers, width):
    group = lane_of((first_ref.shape[0], EDGE)) // GY
    halo = first_ref[:, 3 * width : 3 * width + EDGE].astype(jnp.float32)
    top = pltpu.roll(top_ref[:, 3 * width :].astype(jnp.float32), layers * GY, 1)
    halo = jnp.where(group % (layers + 1) == layers, top, halo)
    return jnp.where(group < 3 * (layers + 1), halo, 0.0).astype(jnp.bfloat16)


def product(a, b):
    return lax.dot_general(a, b, (((1,), (1,)), ((), ())), preferred_element_type=jnp.float32)


def products(held, first, values_ref, image_ref, slot):
    rows = values_ref.shape[0] // 2
    value, image = (ref[slot * rows : (slot + 1) * rows] for ref in (values_ref, image_ref))
    found = []
    for v, i in held:
        both = jnp.dot(image, v[...], preferred_element_type=jnp.float32)
        both += jnp.dot(value, i[...], preferred_element_type=jnp.float32)
        found += [both[:, :rows], both[:, rows:]]
    if slot:
        both = jnp.dot(image, first[0][:, :rows], preferred_element_type=jnp.float32)
        found.append(both + jnp.dot(value, first[1][:, :rows], preferred_element_type=jnp.float32))
    own = product(image, value)
    return [*found, own + own.T]


def fill(layers, width, pieces, top_ref, values_ref):
    depth = 3 * (layers + 1) * width
    copy_in(pieces, 0, values_ref, width)
    values_ref[:, 3 * layers * width : depth] = top_ref[:, : 3 * width]
    values_ref[:, depth:] = halo_of(pieces[0], top_ref, layers, width)


def image_kernel(layers, width, arrays, order, last, *refs):
    refs, (pair, slot) = list(refs), divmod(len(order) - 1, 2)
    place = refs.pop(0) if last else None
    pieces = [refs.pop(0) for _ in range(arrays)]
    top_ref, *matrix, force_ref = (refs.pop(0) for _ in range(5))
    held = [(refs.pop(0), refs.pop(0)) for _ in range(pair)]
    block_refs = [refs.pop(0) for _ in range(len(order) - 1 if last else 0)]
    grad_refs = [refs.pop(0) for _ in range(len(order) - 1 if last else 0)]
    zone_ref = refs.pop(0) if last else None
    first = [refs.pop(0) for _ in range(2 if last else 0)]
    values_ref, image_ref, *outs = refs[(2 if last else 4) * slot :]
    if not last:
        first, outs = outs[:2], outs[2:]
    rows = values_ref.shape[0] // 2
    part = slice(slot * rows, (slot + 1) * rows)
    fill(layers, width, pieces, top_ref, values_ref.at[part])
    image_layers(layers, width, values_ref.at[part], image_ref.at[part], matrix)
    found = products(held, first, values_ref, image_ref, slot)
    nodes = slice(0, 3 * layers * width)
    if not last:
        step = min(2 * TILE, width)
        for start in range(0, values_ref.shape[1], step):
            for ref, to in zip((values_ref, image_ref), first):
                to[start : start + step, part] = ref[part, start : start + step].T
        for j, value in enumerate(found):
            outs[0][j] = value
        outs[1][...] = jnp.dot(force_ref[:, nodes], first[0][nodes, part], preferred_element_type=jnp.float32)[:8]
        return
    grad = product(force_ref[:, nodes], values_ref[part, nodes])[:8]
    keep_ref, send_ref = outs
    half, blocks = rows // 2, len(order)
    pairs = [(i, j) for i in order for j in order]
    lay_out((keep_ref, send_ref), place, half, pairs, blocks_of(order, [*block_refs, found]))
    row = lax.broadcasted_iota(jnp.int32, (blocks, rows), 0)
    small = jnp.zeros((blocks, rows), jnp.float32)
    grads = [*(r[...] for r in grad_refs), grad]
    for name, value in zip(order, grads):
        small = jnp.where(row == (place[0] ^ name), jnp.broadcast_to(value[:1], (blocks, rows)), small)
    for j in range(blocks):
        columns = slice(j * rows, (j + 1) * rows)
        for ref in (keep_ref, send_ref):
            ref[blocks * half : blocks * half + blocks, columns] = small
            ref[blocks * half + blocks :, columns] = zone_ref[...]


def lay_out(refs, place, half, pairs, block):
    for i, j in pairs:
        at = pl.ds(pl.multiple_of((i ^ place[2]) * half, half), half)
        value = block(i, j)
        columns = slice(2 * half * j, 2 * half * (j + 1))
        refs[0][at, columns] = jnp.where(place[1] == 0, value[:half], value[half:])
        refs[1][at, columns] = jnp.where(place[1] == 0, value[half:], value[:half])


def blocks_of(order, block_refs):
    def block(i, j):
        first, second = order.index(i), order.index(j)
        value = block_refs[max(first, second)][min(first, second)]
        return value.T if first < second else value

    return block


def vmem_call(kernel, scalars, args, outs, scratch=(), aliases=None, name="image"):
    vmem = pl.BlockSpec(memory_space=pltpu.VMEM)
    return pl.pallas_call(
        kernel,
        in_specs=[pl.BlockSpec(memory_space=pltpu.SMEM)] * len(scalars) + [vmem] * len(args),
        out_specs=[vmem] * len(outs),
        out_shape=outs,
        scratch_shapes=list(scratch),
        input_output_aliases=aliases or {},
        compiler_params=pltpu.CompilerParams(vmem_limit_bytes=8 << 20),
        cost_estimate=pl.CostEstimate(flops=0, bytes_accessed=16 << 20, transcendentals=0),
        name=name,
    )(*scalars, *args)


def on_device(sensitivity, residual_force, moments, zone_label, misfit):
    cols = sensitivity.shape[1]
    layers = moments.shape[1]
    plane = GX * GY
    n_slab = lax.axis_size("slab")
    n_col = lax.axis_size("col")
    assert n_slab == 2 * n_col
    width = cols * n_col
    source = pltpu.with_memory_space_constraint(sensitivity, pltpu.HBM)
    lanes = plane // n_col
    bottom, total = 3 * lanes + EDGE, 3 * (layers + 1) * lanes + EDGE
    last = n_col - 1
    order = sorted(range(1, n_col), key=lambda k: (k.bit_count(), -k))
    single = [k for k in order if k.bit_count() == 1]
    double = [k for k in order if k.bit_count() > 1 and k != last]
    full = (0, cols)
    calls = [
        [(k, range(layers), full) for k in single],
        [(k, range(layers), full) for k in double]
        + [(last, range(layers // 2), full), (last, range(layers // 2, layers), full)]
        + [(0, range(1), full), (0, range(1, layers), full)],
    ]
    after, pieces = [], {}
    for specs in calls:
        packed, place = pack(source, after, specs, layers, plane, n_col)
        after = [place]
        for (k, _, _), array in zip(specs, packed):
            pieces.setdefault(k, []).append(exchange(array, "col", k) if k else array)
    *matrix, zone = build(moments, zone_label, misfit, residual_force, place, n_col, cols)
    held, blocks, grads, seen = [], [], [], []
    two = pltpu.VMEM((2 * cols, total), jnp.bfloat16)
    wide = pltpu.VMEM((width // 2 + 2 * n_col, width), jnp.float32)
    for k in (0, *order):
        low = crop(pieces[k][0], bottom, blocks[1 if k == last else 0]) if k else pieces[k][0]
        top = shifted(low, "slab", -1)
        slot = len(seen) % 2
        seen.append(k)
        args = [*pieces[k], top, *matrix, *(x for pair in held for x in pair)]
        outs, scalars, aliases = [two, two], [], {}
        if k == last:
            scalars = [place]
            args += [*blocks, *grads, zone, *current[2:]]
            current = current[:2]
            outs += [wide, wide]
        else:
            tall = pltpu.VMEM((total, 2 * cols), jnp.bfloat16)
            outs += [tall, tall, pltpu.VMEM((len(seen), cols, cols), jnp.float32), pltpu.VMEM((8, cols), jnp.float32)]
        if slot:
            aliases = {len(scalars) + len(args) + i: i for i in range(len(current))}
            args += current
        kernel = functools.partial(image_kernel, layers, lanes, len(pieces[k]), tuple(seen), k == last)
        out = vmem_call(kernel, scalars, args, outs, (), aliases)
        if k == last:
            keep, send = out[2:]
        else:
            *current, block, grad = [in_vmem(x) for x in out]
            blocks.append(block)
            grads.append(grad)
            held += [current[2:]] * slot

    mine = keep + exchange(send, "slab", 1)
    parts = [mine[:, k * cols : (k + 1) * cols] for k in range(n_col)]
    mine = parts[0]
    for k in range(1, n_col):
        mine = mine + exchange(parts[k], "col", k)
    half, rows = cols // 2, width // 2
    parts = [jnp.concatenate([mine[k * half : (k + 1) * half], mine[rows:]]) for k in range(n_col)]
    parts = [parts[0]] + [exchange(parts[k], "slab", 2 * k) for k in range(1, n_col)]
    hessian = sum(part[:half] for part in parts).T
    both = sum(part[half:] for part in parts).reshape(2, width)
    gradient = both[0]
    zone_misfit = both[1] * (width / (layers * plane * n_slab))
    return (hessian, gradient, zone_misfit)


def solution(mesh):
    in_specs = (
        P(None, "col", "slab"),
        P(None, "slab"),
        P(None, "slab", None),
        P("slab", None),
        P("slab", None),
    )
    out_specs = (P("col", "slab"), P(), P())
    return jax.shard_map(
        on_device, mesh=mesh, in_specs=in_specs, out_specs=out_specs, check_vma=False
    )
```
